512 devices in a mesh: row: 16 (over y, core), col: 32 (over x, z).
Axes of the slice: x: 4, y: 8, z: 8, core: 2. Of those that a mesh axis runs over, the one named last changes fastest.
Arguments:
- points: float32 [20480, 128], P(('row', 'col')), may hold values from -6 to 6
- source_ids: int32 [20480], P(('row', 'col')), may hold values from 0 to 63
- source_shift: float32 [64, 128], replicated, may hold values from -4 to 4
- noise_level: float32 [64], replicated, may hold values from 0.1 to 1
- weight_in: float32 [128, 256], replicated, may hold values from -0.5 to 0.5
- bias_in: float32 [256], replicated, may hold values from -3 to 3
- weight_out: float32 [256, 32], replicated, may hold values from -0.375 to 0.375
- inverse_scale: float32 [32], replicated, may hold values from 0.15 to 0.6
- frequency: float32 [32, 256], replicated, may hold values from -5 to 5
- phase_shift: float32 [256], replicated, may hold values from -3.140625 to 3.140625
- solution: float32 [20480, 128], P(('row', 'col')), may hold values from -6 to 6
- residual: float32 [20480, 128], P(('row', 'col')), may hold values from -6 to 6
- direction: float32 [20480, 128], P(('row', 'col')), may hold values from -6 to 6
- prior_product: float32 [128], replicated, may hold values from 1280 to 10240
Outputs:
- new_solution: float32 [20480, 128], P(('row', 'col'))
- new_residual: float32 [20480, 128], P(('row', 'col'))
- new_direction: float32 [20480, 128], P(('row', 'col'))
- new_product: float32 [128], replicated
The draws below stay inside these ranges and needn't reach their ends.
All inputs are finite; a program needn't handle non-finite values.
Results may differ from the reference program's by a relative error of at most 0.00024.
Values sent between devices are 32-bit elements; how exact they have to be, the bound alone decides.
No kernel may reach another device: no remote copies, remote signals or barrier semaphores. Data moves between devices by JAX's collectives and lax.ppermute only.
A program may use at most 64 MiB of HBM per device.

```python
import math
import jax
import jax.numpy as jnp
from jax import lax

IN_DIM = 128
HIDDEN_SIZE = 256
FEAT = 32
RHS = 128
RANK = 256
SOURCES = 64
TOTAL = 20480


def plant(drawn, own_key, smallest, largest):
    dims = drawn.shape
    index_at = [jax.random.randint(jax.random.fold_in(own_key, axis), (), 0, dims[axis]) for axis in range(len(dims))]
    drawn = drawn.at[tuple(index_at)].set(smallest)
    longest = dims.index(max(dims))
    index_at[longest] = (index_at[longest] + 1) % dims[longest]
    return drawn.at[tuple(index_at)].set(largest)


def block_scale(rng, shape, split, low, high):
    gain = 1.0
    for dim, blocks in split:
        heights = jax.random.uniform(jax.random.fold_in(jax.random.fold_in(rng, 6), dim), (blocks,), jnp.float32, low / len(split), high / len(split))
        gain = gain * jnp.repeat(jnp.exp(heights), shape[dim] // blocks).reshape((-1,) + (1,) * (len(shape) - 1 - dim))
    return gain


def normal_values(stream_key, dims, scale, reach, cuts=(), kind=jnp.bfloat16):
    result = jax.random.normal(stream_key, dims, jnp.float32) * scale
    if len(cuts) > 0:
        result = block_scale(stream_key, dims, cuts, -0.22, 0.18) * result
    return jnp.clip(result, min=-reach, max=reach).astype(kind)


def setup_inputs(seed: int = 0) -> dict:
    seeds = jax.random.split(jax.random.key(seed), 15)
    points = normal_values(seeds[0], (TOTAL, IN_DIM), 1.0, 6.0, ((0, 512),), jnp.float32)
    source_ids = plant(jax.random.randint(seeds[1], (TOTAL,), 0, SOURCES), jax.random.fold_in(seeds[1], 1), 0, SOURCES - 1).astype(jnp.int32)
    source_shift = normal_values(seeds[2], (SOURCES, IN_DIM), 0.7, 4.0, (), jnp.float32)
    noise_level = jnp.clip(jnp.exp(jax.random.uniform(seeds[3], (SOURCES,), jnp.float32, math.log(0.1), math.log(1.0))), 0.1, 1.0)
    weight_in = normal_values(seeds[4], (IN_DIM, HIDDEN_SIZE), IN_DIM ** -0.5, 0.5, (), jnp.float32)
    bias_in = normal_values(seeds[5], (HIDDEN_SIZE,), 0.7, 3.0, (), jnp.float32)
    weight_out = normal_values(seeds[6], (HIDDEN_SIZE, FEAT), HIDDEN_SIZE ** -0.5, 0.375, (), jnp.float32)
    inverse_scale = jnp.clip(jnp.exp(jax.random.uniform(seeds[7], (FEAT,), jnp.float32, math.log(0.15), math.log(0.6))), 0.15, 0.6)
    frequency = normal_values(seeds[8], (FEAT, RANK), 1.0, 5.0, (), jnp.float32)
    phase_shift = jnp.clip(jax.random.uniform(seeds[9], (RANK,), jnp.float32, -3.140625, 3.140625), -3.140625, 3.140625)
    solution = normal_values(seeds[10], (TOTAL, RHS), 1.0, 6.0, ((0, 512),), jnp.float32)
    residual = normal_values(seeds[11], (TOTAL, RHS), 1.0, 6.0, ((0, 512),), jnp.float32)
    direction = normal_values(seeds[12], (TOTAL, RHS), 1.0, 6.0, ((0, 512),), jnp.float32)
    prior_product = jnp.clip(jnp.exp(jax.random.uniform(seeds[13], (RHS,), jnp.float32, math.log(1280.0), math.log(10240.0))), 1280.0, 10240.0)
    return dict(points=points, source_ids=source_ids, source_shift=source_shift, noise_level=noise_level, weight_in=weight_in, bias_in=bias_in, weight_out=weight_out, inverse_scale=inverse_scale, frequency=frequency, phase_shift=phase_shift, solution=solution, residual=residual, direction=direction, prior_product=prior_product)


HIGH = lax.Precision.HIGHEST

def reference(points, source_ids, source_shift, noise_level, weight_in, bias_in, weight_out, inverse_scale, frequency, phase_shift, solution, residual, direction, prior_product):
    onehot = (source_ids[:, None] == jnp.arange(source_shift.shape[0], dtype=jnp.int32)[None, :]).astype(jnp.float32)
    shifted = points + jnp.dot(onehot, source_shift, precision=HIGH)
    hidden = jnp.tanh(jnp.dot(shifted, weight_in, precision=HIGH) + bias_in)
    scaled = jnp.dot(hidden, weight_out, precision=HIGH) * inverse_scale
    noise = jnp.dot(onehot, noise_level, precision=HIGH)
    squares = lax.optimization_barrier(jnp.sum(scaled * scaled, axis=1))
    total = scaled.shape[0]
    block_rows = math.gcd(total, 1024)
    blocks = scaled.reshape(total // block_rows, block_rows, scaled.shape[1])

    def apply_block(rows_feat):
        row_sq = lax.optimization_barrier(jnp.sum(rows_feat * rows_feat, axis=1))
        distance = row_sq[:, None] + squares[None, :] - 2.0 * jnp.dot(rows_feat, scaled.T, precision=HIGH)
        return jnp.dot(jnp.exp(-0.5 * distance), direction, precision=HIGH)
    kernel_part = lax.map(apply_block, blocks).reshape(total, direction.shape[1])
    image = kernel_part + noise[:, None] * direction
    curvature = lax.optimization_barrier(jnp.sum(direction * image, axis=0))
    alpha = prior_product / curvature
    new_solution = solution + alpha * direction
    new_residual = residual - alpha * image
    rank = frequency.shape[1]
    basis = jnp.sqrt(2.0 / rank) * jnp.cos(jnp.dot(scaled, frequency, precision=HIGH) + phase_shift)
    capacity = jnp.eye(rank, dtype=jnp.float32) + jnp.dot(basis.T, basis / noise[:, None], precision=HIGH)
    projected = jnp.dot(basis.T, new_residual / noise[:, None], precision=HIGH)
    lower = jnp.linalg.cholesky(capacity)
    middle = lax.linalg.triangular_solve(lower, projected, left_side=True, lower=True)
    coeffs = lax.linalg.triangular_solve(lower, middle, left_side=True, lower=True, transpose_a=True)
    precond = (new_residual - jnp.dot(basis, coeffs, precision=HIGH)) / noise[:, None]
    new_product = lax.optimization_barrier(jnp.sum(new_residual * precond, axis=0))
    new_direction = precond + new_product / prior_product * direction
    return (new_solution, new_residual, new_direction, new_product)
```

```python
import jax
import jax.numpy as jnp
from jax import lax
from jax.experimental import pallas as pl
from jax.experimental.pallas import tpu as pltpu
from jax.sharding import Mesh
from jax.sharding import PartitionSpec as P

ROW = ("y", "core")
COL = ("x", "z")
ROW_COL = ("y", "core", "x", "z")
HIGH = lax.Precision.HIGHEST
F32 = jnp.float32
BF16 = jnp.bfloat16
NN = (((1,), (0,)), ((), ()))
NT = (((1,), (1,)), ((), ()))

PI_A = 3.140625
PI_B = 2029.0 / 2**21
PI_C = 1.5099579909783e-07


def call(kernel, outs, *args, flops=1_000_000, scratch=()):
    vmem = pl.BlockSpec(memory_space=pltpu.VMEM)
    return pl.pallas_call(
        kernel,
        out_shape=outs,
        in_specs=[vmem] * len(args),
        out_specs=jax.tree.map(lambda _: vmem, outs),
        scratch_shapes=list(scratch),
        compiler_params=pltpu.CompilerParams(vmem_limit_bytes=48 * 2**20),
        cost_estimate=pl.CostEstimate(flops=flops, bytes_accessed=100_000, transcendentals=0),
    )(*args)


def shape(*dims, dtype=F32):
    return jax.ShapeDtypeStruct(dims, dtype)


def dot(a, b, dims=NN):
    return lax.dot_general(a, b, dims, precision=HIGH, preferred_element_type=F32)


def dot16(a, b, dims=NN):
    return lax.dot_general(a, b, dims, preferred_element_type=F32)


def three(x):
    h = x.astype(BF16).astype(F32)
    m = (x - h).astype(BF16).astype(F32)
    return h, m, (x - h - m).astype(BF16).astype(F32)


def shifted_by(x, lanes):
    return pltpu.roll(x, lanes, 1)


def left_side(x):
    h, m, l = three(x)
    one = h + shifted_by(h, 42) + shifted_by(m, 84)
    two = h + shifted_by(l, 42) + shifted_by(m, 84)
    return jnp.concatenate([one, two], axis=1).astype(BF16)


def right_side(x):
    h, m, l = three(x)
    one = h + shifted_by(m, 42) + shifted_by(h, 84)
    two = l + shifted_by(h, 42) + shifted_by(m, 84)
    return jnp.concatenate([one, two], axis=1).astype(BF16)


def cosine(x):
    turns = jnp.floor(x * (1.0 / 3.141592653589793) + 0.5)
    r = ((x - turns * PI_A) - turns * PI_B) - turns * PI_C
    half = turns * 0.5
    sign = 1.0 - 4.0 * (half - jnp.floor(half))
    s = r * r
    p = 1.0 / 479001600.0
    for c in (-1.0 / 3628800.0, 1.0 / 40320.0, -1.0 / 720.0, 1.0 / 24.0, -0.5, 1.0):
        p = p * s + c
    return sign * p


def lane_of(rows, lanes=128):
    return lax.broadcasted_iota(jnp.int32, (rows, lanes), 1)


def features_kernel(
    points, ids, shift, level, w_in, b_in, w_out, inv, freq, phase, res, drn, to_col, to_row, waves
):
    own = points.shape[0]
    groups = own // 8
    col, row = to_col.shape[0], to_row.shape[0]
    share = res.shape[1] // col
    sources = shift.shape[0]
    hot_t = (lax.broadcasted_iota(jnp.int32, (sources, own), 0) == ids[...]).astype(F32)
    hot = hot_t.T
    shifted = points[...] + dot(hot, shift[...])
    hidden = jnp.tanh(dot(shifted, w_in[...]) + b_in[...])
    f = dot(hidden, w_out[...]) * inv[...]
    n = -0.5 * jnp.sum(f * f, axis=1, keepdims=True)
    noise = dot(jnp.broadcast_to(level[...], (8, sources)), hot_t)
    first = jnp.concatenate([f[8 * g : 8 * g + 8] for g in range(4)], axis=1)
    second = jnp.concatenate(
        [f[8 * g : 8 * g + 8] for g in range(4, groups)]
        + [jnp.zeros((8, own), F32), noise]
        + [n[8 * g : 8 * g + 8] for g in range(groups)]
        + [jnp.zeros((8, 128 - 32 - 2 * own - groups), F32)],
        axis=1,
    )

    def turned(x):
        low, high = jnp.zeros((32, 128), F32), jnp.zeros((128 - 32 - own, 128), F32)
        return jnp.concatenate([low, x, high], axis=0).T

    res_t, drn_t = turned(res[...]), turned(drn[...])
    spare = [jnp.zeros((8 - 2 * share, 128), F32)] if share < 4 else []
    for c in range(col):
        at = slice(c * share, (c + 1) * share)
        to_col[c, :, 0:128] = first
        to_col[c, :, 128:256] = second + jnp.concatenate([res_t[at], drn_t[at]] + spare, axis=0)
    for r in range(row):
        to_row[r, 0:own, :] = drn[...]
        to_row[r, own : own + 8, :] = first
        to_row[r, own + 8 : own + 16, :] = second
    feat = freq.shape[0]
    table = jnp.concatenate(
        [
            freq[...],
            jnp.zeros((1, freq.shape[1]), F32),
            phase[...],
            jnp.zeros((128 - feat - 2, freq.shape[1]), F32),
        ],
        axis=0,
    ).T
    waves[...] = right_side(table)


def unpacked(first, second, x):
    groups = x.shape[1]
    own = groups * 8
    for g in range(groups):
        source = first[:, :, 32 * g : 32 * g + 32] if g < 4 else second[:, :, 32 * g - 128 : 32 * g - 96]
        x[:, g, :, 0:32] = source
        x[:, g, :, 32:33] = second[:, :, 32 + 2 * own + g : 33 + 2 * own + g]
    return x[...].reshape(x.shape[0] * own, 128)


def basis_kernel(arrived, waves, i_side, two_t, noise_row, basis_t, scaled_t, capacity, x):
    pieces, groups = x.shape[0], x.shape[1]
    own = groups * 8
    share = two_t.shape[0] // 2
    values = unpacked(arrived[:, :, 0:128], arrived[:, :, 128:256], x)
    lane = lane_of(values.shape[0])
    values = jnp.where(lane < 33, values, jnp.where(lane == 33, 1.0, 0.0))
    side = left_side(values)
    i_side[...] = side
    for c in range(pieces):
        two_t[:, own * c : own * (c + 1)] = arrived[c, 0 : 2 * share, 160 : 160 + own]
        noise_row[:, own * c : own * (c + 1)] = arrived[c, 0:1, 160 + own : 160 + 2 * own]
    rank = waves.shape[0]
    basis = jnp.sqrt(jnp.float32(2.0 / rank)) * cosine(dot16(waves[...], side, NT))
    weighted = basis / noise_row[...]
    basis_t[...] = basis
    scaled_t[...] = weighted
    capacity[...] = dot(weighted, basis, NT).reshape(capacity.shape)


def products_kernel(arrived, i_side, out, x):
    pieces, groups = x.shape[0], x.shape[1]
    own = groups * 8
    col, share = out.shape[0], out.shape[1]
    values = unpacked(arrived[:, own : own + 8, :], arrived[:, own + 8 : own + 16, :], x)
    lane = lane_of(values.shape[0])
    norm = jnp.where(lane == 32, values, 0.0)
    values = jnp.where(lane < 32, values, jnp.where(lane == 32, 1.0, 0.0)) + shifted_by(norm, 1)
    j_side = right_side(values)
    d_t = arrived[:, 0:own, :].reshape(pieces * own, 128).T
    high = d_t.astype(BF16)
    low = (d_t - high.astype(F32)).astype(BF16)
    both = jnp.concatenate([high, low], axis=0)
    count = i_side.shape[0]
    step = 256
    for i in range(count // step):
        k = jnp.exp(dot16(j_side, i_side[i * step : (i + 1) * step, :], NT))
        k_high = k.astype(BF16)
        k_low = (k - k_high.astype(F32)).astype(BF16)
        pair = dot16(both, k_high)
        total = pair[0:128] + pair[128:256] + dot16(high, k_low)
        for c in range(col):
            out[c, :, i * step : (i + 1) * step] = total[share * c : share * (c + 1)]


def inverse_kernel(pieces, out, work):
    rank = out.shape[0]
    size = 32
    rows = lax.broadcasted_iota(jnp.int32, (rank, rank), 0)
    cols = lax.broadcasted_iota(jnp.int32, (rank, rank), 1)
    work[...] = pieces[...].reshape(rank, rank) + jnp.where(rows == cols, 1.0, 0.0)
    lane = lane_of(size, rank)
    one_lane = lane_of(1, rank)
    sub = lax.broadcasted_iota(jnp.int32, (size, 1), 0)
    for k in range(rank // size):
        base = k * size
        p = work[base : base + size, :]
        for t in range(0, size, 2):
            j = base + t
            r1, r2 = p[t : t + 1, :], p[t + 1 : t + 2, :]
            c1, c2 = p[:, j : j + 1], p[:, j + 1 : j + 2]
            a, b, d = c1[t : t + 1], c2[t : t + 1], c2[t + 1 : t + 2]
            inv = 1.0 / (a * d - b * b)
            first, second = one_lane == j, one_lane == j + 1
            r1 = jnp.where(first, 1.0, jnp.where(second, 0.0, r1))
            r2 = jnp.where(second, 1.0, jnp.where(first, 0.0, r2))
            c1 = jnp.where(sub == t, -1.0, jnp.where(sub == t + 1, 0.0, c1))
            c2 = jnp.where(sub == t + 1, -1.0, jnp.where(sub == t, 0.0, c2))
            u1 = (d * inv) * r1 - (b * inv) * r2
            u2 = (a * inv) * r2 - (b * inv) * r1
            keep = (lane != j) & (lane != j + 1) & (sub != t) & (sub != t + 1)
            p = jnp.where(keep, p, 0.0) - c1 * u1 - c2 * u2
        q = work[:, base : base + size]
        inside = (cols >= base) & (cols < base + size)
        work[...] = jnp.where(inside, 0.0, work[...]) - dot(q, p)
        work[base : base + size, :] = p
    out[...] = work[...]


def sums_kernel(arrived, two_t, noise_row, scaled_t, image, out):
    share = image.shape[0]
    res, drn = two_t[0:share], two_t[share : 2 * share]
    noise = noise_row[...]
    value = jnp.sum(arrived[...], axis=0) + noise * drn
    image[...] = value
    stack = jnp.concatenate([res, value], axis=0)
    proj = dot(stack, scaled_t[...], NT)
    over = value / noise
    left = jnp.concatenate(
        [jnp.sum(res * (res / noise), axis=1, keepdims=True), jnp.sum(value * over, axis=1, keepdims=True)],
        axis=0,
    )
    right = jnp.concatenate(
        [jnp.sum(drn * value, axis=1, keepdims=True), jnp.sum(res * over, axis=1, keepdims=True)],
        axis=0,
    )
    lane = lane_of(2 * share)
    scalars = jnp.where(lane == 0, left, jnp.where(lane == 1, right, 0.0))
    rank = proj.shape[1]
    for r in range(out.shape[0]):
        out[r, :, 0:rank] = proj
        out[r, :, rank : rank + 128] = scalars


def solve_kernel(arrived, prior, inverse, two_t, noise_row, basis_t, image, out):
    share = image.shape[0]
    rank = basis_t.shape[0]
    res, drn = two_t[0:share], two_t[share : 2 * share]
    total = jnp.sum(arrived[...], axis=0)
    scalars = total[:, rank : rank + 2]
    res_res, curvature = scalars[0:share, 0:1], scalars[0:share, 1:2]
    img_img, res_img = scalars[share : 2 * share, 0:1], scalars[share : 2 * share, 1:2]
    alpha = prior[...] / curvature
    projected = total[0:share, 0:rank] - alpha * total[share : 2 * share, 0:rank]
    coeffs = dot(projected, inverse[...])
    norm = res_res - 2.0 * alpha * res_img + alpha * alpha * img_img
    product = norm - jnp.sum(projected * coeffs, axis=1, keepdims=True)
    new_res = res - alpha * image[...]
    precond = (new_res - dot(coeffs, basis_t[...])) / noise_row[...]
    new_drn = precond + product / prior[...] * drn
    pieces = out.shape[0]
    own = new_res.shape[1] // pieces
    spare = jnp.zeros((share, 128 - 2 * own - 2), F32)
    for c in range(pieces):
        at = slice(c * own, (c + 1) * own)
        out[c] = jnp.concatenate([new_res[:, at], new_drn[:, at], alpha, product, spare], axis=1)


def finish_kernel(arrived, solution, direction, new_solution, new_residual, new_direction, new_product):
    own = solution.shape[0]
    t = arrived[...].T
    new_residual[...] = t[0:own]
    new_direction[...] = t[own : 2 * own]
    new_solution[...] = solution[...] + t[2 * own : 2 * own + 1] * direction[...]
    new_product[...] = t[2 * own + 1 : 2 * own + 2]


def exchange(pieces, axes):
    return lax.all_to_all(pieces, axes, split_axis=0, concat_axis=0, tiled=True)


def per_device(
    points,
    source_ids,
    source_shift,
    noise_level,
    weight_in,
    bias_in,
    weight_out,
    inverse_scale,
    frequency,
    phase_shift,
    solution,
    residual,
    direction,
    prior_product,
):
    row, col = lax.axis_size(ROW), lax.axis_size(COL)
    own, columns = direction.shape
    rank = frequency.shape[1]
    groups = own // 8
    share = columns // col
    count = own * col
    prior = lax.dynamic_slice_in_dim(
        prior_product.reshape(columns, 1), lax.axis_index(COL) * share, share, 0
    )
    to_col, to_row, waves = call(
        features_kernel,
        (shape(col, 8, 256), shape(row, own + 16, 128), shape(rank, 256, dtype=BF16)),
        points,
        source_ids.reshape(1, own),
        source_shift,
        noise_level.reshape(1, -1),
        weight_in,
        bias_in.reshape(1, -1),
        weight_out,
        inverse_scale.reshape(1, -1),
        frequency,
        phase_shift.reshape(1, -1),
        residual,
        direction,
    )
    from_col = exchange(to_col, COL)
    from_row = exchange(to_row, ROW)
    i_side, two_t, noise_row, basis_t, scaled_t, capacity = call(
        basis_kernel,
        (
            shape(count, 256, dtype=BF16),
            shape(2 * share, count),
            shape(1, count),
            shape(rank, count),
            shape(rank, count),
            shape(row, rank // row, rank),
        ),
        from_col,
        waves,
        flops=6_000_000_000,
        scratch=[pltpu.VMEM((col, groups, 8, 128), F32)],
    )
    parts = exchange(capacity, ROW)
    products = call(
        products_kernel,
        shape(col, share, count),
        from_row,
        i_side,
        flops=6_000_000_000,
        scratch=[pltpu.VMEM((row, groups, 8, 128), F32)],
    )
    products = exchange(products, COL)
    whole = exchange(
        jnp.broadcast_to(jnp.sum(parts, axis=0), (row, rank // row, rank)), ROW
    )
    image, sums = call(
        sums_kernel,
        (shape(share, count), shape(row, 2 * share, rank + 128)),
        products,
        two_t,
        noise_row,
        scaled_t,
    )
    sums = exchange(sums, ROW)
    inverse = call(
        inverse_kernel,
        shape(rank, rank),
        whole,
        flops=12_000_000_000,
        scratch=[pltpu.VMEM((rank, rank), F32)],
    )
    results = call(
        solve_kernel,
        shape(col, share, 128),
        sums,
        prior,
        inverse,
        two_t,
        noise_row,
        basis_t,
        image,
    )
    results = exchange(results, COL)
    new_solution, new_residual, new_direction, new_product = call(
        finish_kernel,
        (shape(own, columns), shape(own, columns), shape(own, columns), shape(1, columns)),
        results.reshape(columns, 128),
        solution,
        direction,
    )
    return new_solution, new_residual, new_direction, new_product.reshape(columns)


def solution(mesh):
    row, col = mesh.devices.shape
    split = Mesh(mesh.devices.reshape(row // 2, 2, col // 8, 8), ("y", "core", "x", "z"))
    lines = P(ROW_COL, None)
    placed = (lines, P(ROW_COL)) + (P(),) * 8 + (lines, lines, lines, P())
    return jax.shard_map(
        per_device,
        mesh=split,
        in_specs=placed,
        out_specs=(lines, lines, lines, P()),
        check_vma=False,
    )
```

```python
import jax
import jax.numpy as jnp
from jax import lax
from jax.experimental import pallas as pl
from jax.experimental.pallas import tpu as pltpu
from jax.sharding import Mesh
from jax.sharding import PartitionSpec as P

ROW = ("y", "core")
COL = ("x", "z")
ROW_COL = ROW + COL
HIGH = lax.Precision.HIGHEST
F32 = jnp.float32
BF16 = jnp.bfloat16
NN = (((1,), (0,)), ((), ()))
NT = (((1,), (1,)), ((), ()))

PI_A = 3.140625
PI_B = 2029.0 / 2**21
PI_C = 1.5099579909783e-07


def call(kernel, outs, *args, flops=1_000_000, scratch=(), far=(), sent=()):
    vmem, hbm = pl.BlockSpec(memory_space=pltpu.VMEM), pl.BlockSpec(memory_space=pltpu.HBM)
    flat = outs if isinstance(outs, tuple) else (outs,)
    far, sent = list(far), list(sent)
    copied = [args[i] for i in far] + [flat[i] for i in sent]

    def body(*refs):
        ins, res = list(refs[: len(args)]), list(refs[len(args) : len(args) + len(flat)])
        rest = refs[len(args) + len(flat) :]
        rest, held = rest[: len(scratch)], rest[len(scratch) :]
        if not copied:
            return kernel(*ins, *res, *rest)
        held, done = held[:-1], held[-1]
        into = [pltpu.make_async_copy(ins[i], held[n], done.at[n]) for n, i in enumerate(far)]
        for copy in into:
            copy.start()
        for n, i in enumerate(far):
            ins[i] = held[n]
        out = []
        for n, i in enumerate(sent, len(far)):
            out.append(pltpu.make_async_copy(held[n], res[i], done.at[n]))
            res[i] = held[n]
        for copy in into:
            copy.wait()
        kernel(*ins, *res, *rest)
        for copy in out:
            copy.start()
        for copy in out:
            copy.wait()

    extra = [pltpu.VMEM(a.shape, a.dtype) for a in copied]
    if copied:
        extra.append(pltpu.SemaphoreType.DMA((len(copied),)))
    results = pl.pallas_call(
        body,
        out_shape=flat,
        in_specs=[hbm if i in far else vmem for i in range(len(args))],
        out_specs=tuple(hbm if i in sent else vmem for i in range(len(flat))),
        scratch_shapes=list(scratch) + extra,
        compiler_params=pltpu.CompilerParams(vmem_limit_bytes=(63 if far else 16) * 2**20),
        cost_estimate=pl.CostEstimate(flops=flops, bytes_accessed=100_000, transcendentals=0),
    )(*args)
    return results if isinstance(outs, tuple) else results[0]


def shape(*dims, dtype=F32):
    return jax.ShapeDtypeStruct(dims, dtype)


def dot(a, b, dims=NN):
    return lax.dot_general(a, b, dims, precision=HIGH, preferred_element_type=F32)


def dot16(a, b, dims=NN):
    return lax.dot_general(a, b, dims, preferred_element_type=F32)


def three(x):
    h = x.astype(BF16).astype(F32)
    m = (x - h).astype(BF16).astype(F32)
    return h, m, (x - h - m).astype(BF16).astype(F32)


def shifted_by(x, lanes):
    return pltpu.roll(x, lanes, 1)


def left_side(x):
    h, m, l = three(x)
    one = h + shifted_by(h, 42) + shifted_by(m, 84)
    two = h + shifted_by(l, 42) + shifted_by(m, 84)
    return jnp.concatenate([one, two], axis=1).astype(BF16)


def right_side(x):
    h, m, l = three(x)
    one = h + shifted_by(m, 42) + shifted_by(h, 84)
    two = l + shifted_by(h, 42) + shifted_by(m, 84)
    return jnp.concatenate([one, two], axis=1).astype(BF16)


def cosine(x):
    turns = jnp.floor(x * (1.0 / 3.141592653589793) + 0.5)
    r = ((x - turns * PI_A) - turns * PI_B) - turns * PI_C
    half = turns * 0.5
    sign = 1.0 - 4.0 * (half - jnp.floor(half))
    s = r * r
    p = 1.0 / 479001600.0
    for c in (-1.0 / 3628800.0, 1.0 / 40320.0, -1.0 / 720.0, 1.0 / 24.0, -0.5, 1.0):
        p = p * s + c
    return sign * p


def lane_of(rows, lanes=128):
    return lax.broadcasted_iota(jnp.int32, (rows, lanes), 1)


def features_kernel(
    points, ids, shift, level, w_in, b_in, w_out_t, inv, freq, phase, res, drn, prior, to_row, to_col, waves
):
    own = points.shape[0]
    groups = own // 8
    sources = shift.shape[0]
    hot_t = (lax.broadcasted_iota(jnp.int32, (sources, own), 0) == ids[...]).astype(F32)
    hot = hot_t.T
    shifted = points[...] + dot(hot, shift[...])
    hidden = jnp.tanh(dot(shifted, w_in[...]) + b_in[...])
    f = dot(hidden, w_out_t[...], NT) * inv[...]
    n = -0.5 * jnp.sum(f * f, axis=1, keepdims=True)
    noise = dot(jnp.broadcast_to(level[...], (8, sources)), hot_t)
    first = jnp.concatenate([f[8 * g : 8 * g + 8] for g in range(4)], axis=1)
    second = jnp.concatenate(
        [f[8 * g : 8 * g + 8] for g in range(4, groups)]
        + [jnp.zeros((8, own), F32), noise]
        + [n[8 * g : 8 * g + 8] for g in range(groups)]
        + [jnp.zeros((8, 128 - 32 - 2 * own - groups), F32)],
        axis=1,
    )
    to_row[0:own, :] = drn[...]
    to_row[own : own + 8, :] = first
    to_row[own + 8 : own + 16, :] = second
    col = to_col.shape[0]
    share = res.shape[1] // col

    def turned(x):
        low, high = jnp.zeros((32, 128), F32), jnp.zeros((128 - 32 - own, 128), F32)
        return jnp.concatenate([low, x, high], axis=0).T

    prior_t = jnp.broadcast_to(prior[...], (128, 128)).T
    res_t = jnp.where(lane_of(128) == 32 + 2 * own + groups, prior_t, turned(res[...]))
    drn_t = turned(drn[...])
    spare = [jnp.zeros((8 - 2 * share, 128), F32)] if share < 4 else []
    for c in range(col):
        at = slice(c * share, (c + 1) * share)
        to_col[c, :, 0:128] = first
        to_col[c, :, 128:256] = second + jnp.concatenate([res_t[at], drn_t[at]] + spare, axis=0)
    feat = freq.shape[0]
    table = jnp.concatenate(
        [
            freq[...],
            jnp.zeros((1, freq.shape[1]), F32),
            phase[...],
            jnp.zeros((128 - feat - 2, freq.shape[1]), F32),
        ],
        axis=0,
    ).T
    waves[...] = right_side(table)


def unpacked(first, second, x):
    groups = x.shape[1]
    own = groups * 8
    for g in range(groups):
        source = first[:, :, 32 * g : 32 * g + 32] if g < 4 else second[:, :, 32 * g - 128 : 32 * g - 96]
        x[:, g, :, 0:32] = source
        x[:, g, :, 32:33] = second[:, :, 32 + 2 * own + g : 33 + 2 * own + g]
    return x[...].reshape(x.shape[0] * own, 128)


def basis_kernel(arrived, waves, i_side, two_t, noise_row, prior, basis_t, capacity, x):
    pieces, groups = x.shape[0], x.shape[1]
    own = groups * 8
    share = two_t.shape[0] // 2
    values = unpacked(arrived[:, :, 0:128], arrived[:, :, 128:256], x)
    lane = lane_of(values.shape[0])
    values = jnp.where(lane < 33, values, jnp.where(lane == 33, 1.0, 0.0))
    side = left_side(values)
    i_side[...] = side
    for c in range(pieces):
        two_t[:, own * c : own * (c + 1)] = arrived[c, 0 : 2 * share, 160 : 160 + own]
        noise_row[:, own * c : own * (c + 1)] = arrived[c, 0:1, 160 + own : 160 + 2 * own]
    at = 160 + 2 * own + groups
    prior[...] = arrived[0, 0:share, at : at + 1]
    rank = waves.shape[0]
    basis = jnp.sqrt(jnp.float32(2.0 / rank)) * cosine(dot16(waves[...], side, NT))
    weighted = basis / noise_row[...]
    basis_t[...] = basis
    capacity[...] = dot(weighted, basis, NT).reshape(capacity.shape)


def products_kernel(arrived, i_side, out, x):
    pieces, groups = x.shape[0], x.shape[1]
    own = groups * 8
    col, share = out.shape[0], out.shape[1]
    values = unpacked(arrived[:, own : own + 8, :], arrived[:, own + 8 : own + 16, :], x)
    lane = lane_of(values.shape[0])
    norm = jnp.where(lane == 32, values, 0.0)
    values = jnp.where(lane < 32, values, jnp.where(lane == 32, 1.0, 0.0)) + shifted_by(norm, 1)
    j_side = right_side(values)
    d_t = arrived[:, 0:own, :].reshape(pieces * own, 128).T
    d_high, d_mid, d_low = three(d_t)
    all_three = jnp.concatenate([d_high, d_mid, d_low], axis=0).astype(BF16)
    wide = d_t.shape[0]
    count = i_side.shape[0]
    step = 256
    for i in range(count // step):
        k = jnp.exp(dot16(j_side, i_side[i * step : (i + 1) * step, :], NT))
        k_high = k.astype(BF16)
        left = k - k_high.astype(F32)
        k_mid = left.astype(BF16)
        k_low = (left - k_mid.astype(F32)).astype(BF16)
        by_mid = dot16(all_three[0 : 2 * wide], k_mid)
        by_high = dot16(all_three, k_high)
        total = dot16(all_three[0:wide], k_low) + by_mid[wide:] + by_high[2 * wide :]
        total = by_high[0:wide] + (by_high[wide : 2 * wide] + by_mid[0:wide] + total)
        for c in range(col):
            out[c, :, i * step : (i + 1) * step] = total[share * c : share * (c + 1)]


def whole_kernel(parts, out):
    out[...] = jnp.sum(parts[...], axis=0)


def eliminated(p, base, lane, one_lane, sub):
    size, rank = p.shape
    for t in range(0, size, 4):
        j = base + t
        c = [jnp.broadcast_to(p[:, j + i : j + i + 1], (size, rank)) for i in range(4)]
        s = [[c[i][t + q : t + q + 1] for q in range(4)] for i in range(4)]
        inside = (one_lane >= j) & (one_lane < j + 4)
        r = [
            jnp.where(inside, jnp.where(one_lane == j + i, 1.0, 0.0), p[t + i : t + i + 1])
            for i in range(4)
        ]
        inv = 1.0 / (s[0][0] * s[1][1] - s[0][1] * s[0][1])
        a0, a1, a2 = s[1][1] * inv, -s[0][1] * inv, s[0][0] * inv
        g02, g03 = a0 * s[2][0] + a1 * s[2][1], a0 * s[3][0] + a1 * s[3][1]
        g12, g13 = a1 * s[2][0] + a2 * s[2][1], a1 * s[3][0] + a2 * s[3][1]
        e = s[2][2] - s[2][0] * g02 - s[2][1] * g12
        f = s[3][2] - s[2][0] * g03 - s[2][1] * g13
        h = s[3][3] - s[3][0] * g03 - s[3][1] * g13
        inv = 1.0 / (e * h - f * f)
        e, f, h = h * inv, -f * inv, e * inv
        v2 = r[2] - g02 * r[0] - g12 * r[1]
        v3 = r[3] - g03 * r[0] - g13 * r[1]
        u2 = e * v2 + f * v3
        u3 = f * v2 + h * v3
        u0 = a0 * r[0] + a1 * r[1] - g02 * u2 - g03 * u3
        u1 = a1 * r[0] + a2 * r[1] - g12 * u2 - g13 * u3
        here = (sub >= t) & (sub < t + 4)
        p = jnp.where(((lane < j) | (lane >= j + 4)) & ~here, p, 0.0)
        for i, u in enumerate((u0, u1, u2, u3)):
            p = p - jnp.where(here, jnp.where(sub == t + i, -1.0, 0.0), c[i]) * u
    return p


def inverse_kernel(gram, out):
    rank = out.shape[0]
    size = 32
    rows = lax.broadcasted_iota(jnp.int32, (rank, rank), 0)
    cols = lax.broadcasted_iota(jnp.int32, (rank, rank), 1)
    m = gram[...] + jnp.where(rows == cols, 1.0, 0.0)
    count = rank // size
    panels = [m[i * size : (i + 1) * size] for i in range(count)]
    lane, one_lane = lane_of(size, rank), lane_of(1, rank)
    sub = lax.broadcasted_iota(jnp.int32, (size, rank), 0)
    for k in range(count):
        base = k * size
        p = eliminated(panels[k], base, lane, one_lane, sub)
        panels[k] = p

        def updated(x):
            at = lane_of(x.shape[0], rank)
            inside = (at >= base) & (at < base + size)
            return jnp.where(inside, 0.0, x) - dot(x[:, base : base + size], p)

        others = [i for i in range(count) if i != k]
        if k + 1 < count:
            panels[k + 1] = updated(panels[k + 1])
            others.remove(k + 1)
        rest = updated(jnp.concatenate([panels[i] for i in others], axis=0))
        for w, i in enumerate(others):
            panels[i] = rest[w * size : (w + 1) * size]
    for i in range(count):
        out[i * size : (i + 1) * size] = panels[i]


def sums_kernel(arrived, two_t, noise_row, basis_t, image, out):
    share = image.shape[0]
    res, drn = two_t[0:share], two_t[share : 2 * share]
    noise = noise_row[...]
    value = jnp.sum(arrived[...], axis=0) + noise * drn
    image[...] = value
    stack = jnp.concatenate([res, value], axis=0)
    scaled = stack / noise
    proj = dot(scaled, basis_t[...], NT)
    over = scaled[share:]
    left = jnp.concatenate(
        [jnp.sum(res * scaled[0:share], axis=1, keepdims=True), jnp.sum(value * over, axis=1, keepdims=True)],
        axis=0,
    )
    right = jnp.concatenate(
        [jnp.sum(drn * value, axis=1, keepdims=True), jnp.sum(res * over, axis=1, keepdims=True)],
        axis=0,
    )
    lane = lane_of(2 * share)
    scalars = jnp.where(lane == 0, left, jnp.where(lane == 1, right, 0.0))
    rank = proj.shape[1]
    for r in range(out.shape[0]):
        out[r, :, 0:rank] = proj
        out[r, :, rank : rank + 128] = scalars


def solve_kernel(arrived, prior, inverse, gram, two_t, noise_row, basis_t, image, out):
    share = image.shape[0]
    rank = basis_t.shape[0]
    res, drn = two_t[0:share], two_t[share : 2 * share]
    total = jnp.sum(arrived[...], axis=0)
    scalars = total[:, rank : rank + 2]
    res_res, curvature = scalars[0:share, 0:1], scalars[0:share, 1:2]
    img_img, res_img = scalars[share : 2 * share, 0:1], scalars[share : 2 * share, 1:2]
    alpha = prior[...] / curvature
    projected = total[0:share, 0:rank] - alpha * total[share : 2 * share, 0:rank]
    coeffs = dot(projected, inverse[...])
    coeffs = coeffs + dot(projected - coeffs - dot(coeffs, gram[...]), inverse[...])
    norm = res_res - 2.0 * alpha * res_img + alpha * alpha * img_img
    product = norm - jnp.sum(projected * coeffs, axis=1, keepdims=True)
    new_res = res - alpha * image[...]
    precond = (new_res - dot(coeffs, basis_t[...])) / noise_row[...]
    new_drn = precond + product / prior[...] * drn
    pieces = out.shape[0]
    own = new_res.shape[1] // pieces
    spare = jnp.zeros((share, 128 - 2 * own - 2), F32)
    for c in range(pieces):
        at = slice(c * own, (c + 1) * own)
        out[c] = jnp.concatenate([new_res[:, at], new_drn[:, at], alpha, product, spare], axis=1)


def finish_kernel(arrived, solution, direction, new_solution, new_residual, new_direction, new_product):
    own = solution.shape[0]
    t = arrived[...].T
    new_residual[...] = t[0:own]
    new_direction[...] = t[own : 2 * own]
    new_solution[...] = solution[...] + t[2 * own : 2 * own + 1] * direction[...]
    new_product[...] = t[2 * own + 1 : 2 * own + 2]


def exchange(pieces, axes):
    return lax.all_to_all(pieces, axes, split_axis=0, concat_axis=0, tiled=True)


def per_device(
    points,
    source_ids,
    source_shift,
    noise_level,
    weight_in,
    bias_in,
    weight_out,
    inverse_scale,
    frequency,
    phase_shift,
    solution,
    residual,
    direction,
    prior_product,
):
    row, col = lax.axis_size(ROW), lax.axis_size(COL)
    own, columns = direction.shape
    rank = frequency.shape[1]
    groups = own // 8
    share = columns // col
    count = own * col
    to_row, to_col, waves = call(
        features_kernel,
        (shape(own + 16, 128), shape(col, 8, 256), shape(rank, 256, dtype=BF16)),
        points,
        source_ids.reshape(1, own),
        source_shift,
        noise_level.reshape(1, -1),
        weight_in,
        bias_in.reshape(1, -1),
        weight_out.T,
        inverse_scale.reshape(1, -1),
        frequency,
        phase_shift.reshape(1, -1),
        residual,
        direction,
        prior_product.reshape(1, -1),
        far=range(13),
        sent=(1,),
    )
    from_col = exchange(to_col, COL)
    from_row = lax.all_gather(to_row, ROW, axis=0, tiled=False)
    i_side, two_t, noise_row, prior, basis_t, capacity = call(
        basis_kernel,
        (
            shape(count, 256, dtype=BF16),
            shape(2 * share, count),
            shape(1, count),
            shape(share, 1),
            shape(rank, count),
            shape(row, rank // row, rank),
        ),
        from_col,
        waves,
        flops=6_000_000_000,
        sent=(5,),
        scratch=[pltpu.VMEM((col, groups, 8, 128), F32)],
    )
    parts = exchange(capacity, ROW)
    products = call(
        products_kernel,
        shape(col, share, count),
        from_row,
        i_side,
        flops=6_000_000_000,
        sent=(0,),
        scratch=[pltpu.VMEM((row, groups, 8, 128), F32)],
    )
    products = exchange(products, COL)
    own_rows = call(whole_kernel, shape(rank // row, rank), parts)
    whole = lax.all_gather(own_rows, ROW, axis=0, tiled=True)
    image, sums = call(
        sums_kernel,
        (shape(share, count), shape(row, 2 * share, rank + 128)),
        products,
        two_t,
        noise_row,
        basis_t,
        sent=(1,),
    )
    sums = exchange(sums, ROW)
    inverse = call(
        inverse_kernel,
        shape(rank, rank),
        whole,
        flops=12_000_000_000,
    )
    results = call(
        solve_kernel,
        shape(col, share, 128),
        sums,
        prior,
        inverse,
        whole,
        two_t,
        noise_row,
        basis_t,
        image,
    )
    results = exchange(results, COL)
    new_solution, new_residual, new_direction, new_product = call(
        finish_kernel,
        (shape(own, columns), shape(own, columns), shape(own, columns), shape(1, columns)),
        results.reshape(columns, 128),
        solution,
        direction,
        far=(1, 2),
        sent=(0, 1, 2),
    )
    return new_solution, new_residual, new_direction, new_product.reshape(columns)


def solution(mesh):
    row, col = mesh.devices.shape
    split = Mesh(mesh.devices.reshape(row // 2, 2, col // 8, 8), ROW_COL)
    lines = P(ROW_COL, None)
    placed = (lines, P(ROW_COL)) + (P(),) * 8 + (lines, lines, lines, P())
    return jax.shard_map(
        per_device,
        mesh=split,
        in_specs=placed,
        out_specs=(lines, lines, lines, P()),
        check_vma=False,
    )
```

```python
import jax
import jax.numpy as jnp
from jax import lax
from jax.experimental import pallas as pl
from jax.experimental.pallas import tpu as pltpu
from jax.sharding import Mesh
from jax.sharding import PartitionSpec as P

ROW = ("y", "core")
COL = ("x", "z")
ROW_COL = ROW + COL
HIGH = lax.Precision.HIGHEST
F32 = jnp.float32
BF16 = jnp.bfloat16
NN = (((1,), (0,)), ((), ()))
NT = (((1,), (1,)), ((), ()))

PI_A = 3.140625
PI_B = 2029.0 / 2**21
PI_C = 1.5099579909783e-07


def call(kernel, outs, *args, flops=1_000_000, scratch=(), far=(), sent=()):
    vmem, hbm = pl.BlockSpec(memory_space=pltpu.VMEM), pl.BlockSpec(memory_space=pltpu.HBM)
    flat = outs if isinstance(outs, tuple) else (outs,)
    far, sent = list(far), list(sent)
    copied = [args[i] for i in far] + [flat[i] for i in sent]

    def body(*refs):
        ins, res = list(refs[: len(args)]), list(refs[len(args) : len(args) + len(flat)])
        rest = refs[len(args) + len(flat) :]
        rest, held = rest[: len(scratch)], rest[len(scratch) :]
        if not copied:
            return kernel(*ins, *res, *rest)
        held, done = held[:-1], held[-1]
        into = [pltpu.make_async_copy(ins[i], held[n], done.at[n]) for n, i in enumerate(far)]
        for copy in into:
            copy.start()
        for n, i in enumerate(far):
            ins[i] = held[n]
        out = []
        for n, i in enumerate(sent, len(far)):
            out.append(pltpu.make_async_copy(held[n], res[i], done.at[n]))
            res[i] = held[n]
        for copy in into:
            copy.wait()
        kernel(*ins, *res, *rest)
        for copy in out:
            copy.start()
        for copy in out:
            copy.wait()

    extra = [pltpu.VMEM(a.shape, a.dtype) for a in copied]
    if copied:
        extra.append(pltpu.SemaphoreType.DMA((len(copied),)))
    results = pl.pallas_call(
        body,
        out_shape=flat,
        in_specs=[hbm if i in far else vmem for i in range(len(args))],
        out_specs=tuple(hbm if i in sent else vmem for i in range(len(flat))),
        scratch_shapes=list(scratch) + extra,
        compiler_params=pltpu.CompilerParams(vmem_limit_bytes=(63 if far else 16) * 2**20),
        cost_estimate=pl.CostEstimate(flops=flops, bytes_accessed=100_000, transcendentals=0),
    )(*args)
    return results if isinstance(outs, tuple) else results[0]


def shape(*dims, dtype=F32):
    return jax.ShapeDtypeStruct(dims, dtype)


def dot(a, b, dims=NN):
    return lax.dot_general(a, b, dims, precision=HIGH, preferred_element_type=F32)


def dot16(a, b, dims=NN):
    return lax.dot_general(a, b, dims, preferred_element_type=F32)


def three(x):
    h = x.astype(BF16).astype(F32)
    m = (x - h).astype(BF16).astype(F32)
    return h, m, (x - h - m).astype(BF16).astype(F32)


def stacked(x, b3, dims):
    h, m, l = three(x)
    none = jnp.zeros_like(x)
    by_h = dot16(jnp.concatenate([h, m, l, none], axis=0).astype(BF16), b3[0], dims)
    by_m = dot16(jnp.concatenate([h, m], axis=0).astype(BF16), b3[1], dims)
    by_l = dot16(jnp.concatenate([h, none], axis=0).astype(BF16), b3[2], dims)
    return by_h[0:8] + (by_h[8:16] + by_m[0:8] + (by_h[16:24] + by_m[8:16] + by_l[0:8]))


def shifted_by(x, lanes):
    return pltpu.roll(x, lanes, 1)


def left_side(x):
    h, m, l = three(x)
    one = h + shifted_by(h, 42) + shifted_by(m, 84)
    two = h + shifted_by(l, 42) + shifted_by(m, 84)
    return jnp.concatenate([one, two], axis=1).astype(BF16)


def right_side(x):
    h, m, l = three(x)
    one = h + shifted_by(m, 42) + shifted_by(h, 84)
    two = l + shifted_by(h, 42) + shifted_by(m, 84)
    return jnp.concatenate([one, two], axis=1).astype(BF16)


def cosine(x):
    turns = jnp.floor(x * (1.0 / 3.141592653589793) + 0.5)
    r = ((x - turns * PI_A) - turns * PI_B) - turns * PI_C
    half = turns * 0.5
    sign = 1.0 - 4.0 * (half - jnp.floor(half))
    s = r * r
    p = 1.0 / 479001600.0
    for c in (-1.0 / 3628800.0, 1.0 / 40320.0, -1.0 / 720.0, 1.0 / 24.0, -0.5, 1.0):
        p = p * s + c
    return sign * p


def lane_of(rows, lanes=128):
    return lax.broadcasted_iota(jnp.int32, (rows, lanes), 1)


def features_kernel(
    points, ids, shift, level, w_in, b_in, w_out_t, inv, freq, phase, res, drn, prior, to_row, to_col, waves
):
    own = points.shape[0]
    groups = own // 8
    sources = shift.shape[0]
    hot_t = (lax.broadcasted_iota(jnp.int32, (sources, own), 0) == ids[...]).astype(F32)
    hot = hot_t.T
    shifted = points[...] + dot(hot, shift[...])
    hidden = jnp.tanh(dot(shifted, w_in[...]) + b_in[...])
    f = dot(hidden, w_out_t[...], NT) * inv[...]
    n = -0.5 * jnp.sum(f * f, axis=1, keepdims=True)
    noise = dot(hot, jnp.broadcast_to(level[...], (8, sources)), NT)[:, 0:1]
    first = jnp.concatenate([f[8 * g : 8 * g + 8] for g in range(4)], axis=1)
    second = jnp.concatenate(
        [f[8 * g : 8 * g + 8] for g in range(4, groups)]
        + [jnp.zeros((8, own), F32)]
        + [x[8 * g : 8 * g + 8] for g in range(groups) for x in (n, noise)]
        + [jnp.zeros((8, 128 - 32 - own - 2 * groups), F32)],
        axis=1,
    )
    to_row[0:own, :] = drn[...]
    to_row[own : own + 8, :] = first
    to_row[own + 8 : own + 16, :] = second
    col = to_col.shape[0]
    share = res.shape[1] // col

    def turned(x):
        low, high = jnp.zeros((32, 128), F32), jnp.zeros((128 - 32 - own, 128), F32)
        return jnp.concatenate([low, x, high], axis=0).T

    prior_t = jnp.broadcast_to(prior[...], (128, 128)).T
    res_t = jnp.where(lane_of(128) == 32 + own + 2 * groups, prior_t, turned(res[...]))
    drn_t = turned(drn[...])
    spare = [jnp.zeros((8 - 2 * share, 128), F32)] if share < 4 else []
    for c in range(col):
        at = slice(c * share, (c + 1) * share)
        to_col[c, :, 0:128] = first
        to_col[c, :, 128:256] = second + jnp.concatenate([res_t[at], drn_t[at]] + spare, axis=0)
    feat = freq.shape[0]
    rank = freq.shape[1]
    table = jnp.concatenate(
        [
            freq[...],
            jnp.zeros((2, rank), F32),
            phase[...],
            jnp.zeros((128 - feat - 3, rank), F32),
        ],
        axis=0,
    ).T
    pick = jnp.where(lane_of(waves.shape[0] - rank) == feat + 1, 1.0, 0.0)
    waves[...] = right_side(jnp.concatenate([table, pick], axis=0))


def unpacked(first, second, x):
    groups = x.shape[1]
    own = groups * 8
    for g in range(groups):
        source = first[:, :, 32 * g : 32 * g + 32] if g < 4 else second[:, :, 32 * g - 128 : 32 * g - 96]
        x[:, g, :, 0:32] = source
        at = 32 + own + 2 * g
        x[:, g, :, 32:34] = second[:, :, at : at + 2]
    return x[...].reshape(x.shape[0] * own, 128)


def basis_kernel(arrived, waves, i_side, two_t, noise_row, prior, basis_3, capacity, x):
    groups = x.shape[1]
    own = groups * 8
    share = prior.shape[0]
    values = unpacked(arrived[:, :, 0:128], arrived[:, :, 128:256], x)
    lane = lane_of(values.shape[0])
    values = jnp.where(lane < 34, values, jnp.where(lane == 34, 1.0, 0.0))
    side = left_side(values)
    i_side[...] = side
    for c in range(arrived.shape[0]):
        two_t[:, own * c : own * (c + 1)] = arrived[c, 0 : 2 * share, 160 : 160 + own]
    at = 160 + own + 2 * groups
    prior[...] = arrived[0, 0:share, at : at + 1]
    rank = basis_3.shape[1]
    half = rank // 2
    turned = dot16(waves[...], side, NT)
    noise = turned[rank : rank + 1]
    noise_row[...] = noise
    basis = jnp.sqrt(jnp.float32(2.0 / rank)) * cosine(turned[0:rank])
    h, m, l = three(basis)
    basis_3[0], basis_3[1], basis_3[2] = h.astype(BF16), m.astype(BF16), l.astype(BF16)
    weighted = basis * (1.0 / noise)
    upper = dot(weighted[0:half], basis[0:half], NT)
    lower = dot(weighted[half:], basis, NT)
    blocks = jnp.concatenate([upper, lower[:, 0:half], lower[:, half:]], axis=0)
    capacity[...] = blocks.reshape(capacity.shape)


def products_kernel(arrived, i_side, out, x):
    pieces, groups = x.shape[0], x.shape[1]
    own = groups * 8
    col, share = out.shape[0], out.shape[1]
    values = unpacked(arrived[:, own : own + 8, :], arrived[:, own + 8 : own + 16, :], x)
    lane = lane_of(values.shape[0])
    norm = jnp.where(lane == 32, values, 0.0)
    values = jnp.where(lane < 32, values, jnp.where(lane == 32, 1.0, 0.0)) + shifted_by(norm, 2)
    j_side = right_side(values)
    d_t = arrived[:, 0:own, :].reshape(pieces * own, 128).T
    high = d_t.astype(BF16)
    low = (d_t - high.astype(F32)).astype(BF16)
    both = jnp.concatenate([high, low], axis=0)
    count = i_side.shape[0]
    step = 256
    for i in range(count // step):
        k = jnp.exp(dot16(j_side, i_side[i * step : (i + 1) * step, :], NT))
        k_high = k.astype(BF16)
        k_low = (k - k_high.astype(F32)).astype(BF16)
        pair = dot16(both, k_high)
        total = pair[0:128] + (pair[128:256] + dot16(high, k_low))
        for c in range(col):
            out[c, :, i * step : (i + 1) * step] = total[share * c : share * (c + 1)]


def whole_kernel(parts, out):
    out[...] = jnp.sum(parts[...], axis=0)


def eliminated(p, base, lane, one_lane, sub):
    size, rank = p.shape
    for t in range(0, size, 4):
        j = base + t
        c = [jnp.broadcast_to(p[:, j + i : j + i + 1], (size, rank)) for i in range(4)]
        s = [[c[i][t + q : t + q + 1] for q in range(4)] for i in range(4)]
        inside = (one_lane >= j) & (one_lane < j + 4)
        r = [
            jnp.where(inside, jnp.where(one_lane == j + i, 1.0, 0.0), p[t + i : t + i + 1])
            for i in range(4)
        ]
        inv = 1.0 / (s[0][0] * s[1][1] - s[0][1] * s[0][1])
        a0, a1, a2 = s[1][1] * inv, -s[0][1] * inv, s[0][0] * inv
        g02, g03 = a0 * s[2][0] + a1 * s[2][1], a0 * s[3][0] + a1 * s[3][1]
        g12, g13 = a1 * s[2][0] + a2 * s[2][1], a1 * s[3][0] + a2 * s[3][1]
        e = s[2][2] - s[2][0] * g02 - s[2][1] * g12
        f = s[3][2] - s[2][0] * g03 - s[2][1] * g13
        h = s[3][3] - s[3][0] * g03 - s[3][1] * g13
        inv = 1.0 / (e * h - f * f)
        e, f, h = h * inv, -f * inv, e * inv
        v2 = r[2] - g02 * r[0] - g12 * r[1]
        v3 = r[3] - g03 * r[0] - g13 * r[1]
        u2 = e * v2 + f * v3
        u3 = f * v2 + h * v3
        u0 = a0 * r[0] + a1 * r[1] - g02 * u2 - g03 * u3
        u1 = a1 * r[0] + a2 * r[1] - g12 * u2 - g13 * u3
        here = (sub >= t) & (sub < t + 4)
        p = jnp.where(((lane < j) | (lane >= j + 4)) & ~here, p, 0.0)
        for i, u in enumerate((u0, u1, u2, u3)):
            p = p - jnp.where(here, jnp.where(sub == t + i, -1.0, 0.0), c[i]) * u
    return p


def inverse_kernel(blocks, out, gram):
    rank = out.shape[0]
    size = 32
    rows = lax.broadcasted_iota(jnp.int32, (rank, rank), 0)
    cols = lax.broadcasted_iota(jnp.int32, (rank, rank), 1)
    half = rank // 2
    one, two, three_ = blocks[0:half], blocks[half:rank], blocks[rank : rank + half]
    m = jnp.concatenate(
        [jnp.concatenate([one, two.T], axis=1), jnp.concatenate([two, three_], axis=1)], axis=0
    )
    m = m + jnp.where(rows == cols, 1.0, 0.0)
    gram[...] = m
    count = rank // size
    panels = [m[i * size : (i + 1) * size] for i in range(count)]
    lane, one_lane = lane_of(size, rank), lane_of(1, rank)
    sub = lax.broadcasted_iota(jnp.int32, (size, rank), 0)
    for k in range(count):
        base = k * size
        p = eliminated(panels[k], base, lane, one_lane, sub)
        panels[k] = p

        def updated(x):
            at = lane_of(x.shape[0], rank)
            inside = (at >= base) & (at < base + size)
            return jnp.where(inside, 0.0, x) - dot(x[:, base : base + size], p)

        others = [i for i in range(count) if i != k]
        if k + 1 < count:
            panels[k + 1] = updated(panels[k + 1])
            others.remove(k + 1)
        rest = updated(jnp.concatenate([panels[i] for i in others], axis=0))
        for w, i in enumerate(others):
            panels[i] = rest[w * size : (w + 1) * size]
    for i in range(count):
        out[i * size : (i + 1) * size] = panels[i]


def sums_kernel(arrived, two_t, noise_row, basis_3, image, out):
    share = image.shape[0]
    res, drn = two_t[0:share], two_t[share : 2 * share]
    noise = noise_row[...]
    value = jnp.sum(arrived[...], axis=0) + noise * drn
    image[...] = value
    stack = jnp.concatenate([res, value], axis=0)
    scaled = stack * (1.0 / noise)
    proj = stacked(scaled, basis_3, NT)
    over = scaled[share:]
    left = jnp.concatenate(
        [jnp.sum(res * scaled[0:share], axis=1, keepdims=True), jnp.sum(value * over, axis=1, keepdims=True)],
        axis=0,
    )
    right = jnp.concatenate(
        [jnp.sum(drn * value, axis=1, keepdims=True), jnp.sum(res * over, axis=1, keepdims=True)],
        axis=0,
    )
    lane = lane_of(2 * share)
    scalars = jnp.where(lane == 0, left, jnp.where(lane == 1, right, 0.0))
    rank = proj.shape[1]
    for r in range(out.shape[0]):
        out[r, :, 0:rank] = proj
        out[r, :, rank : rank + 128] = scalars


def solve_kernel(arrived, prior, inverse, gram, two_t, noise_row, basis_3, image, out):
    share = image.shape[0]
    rank = gram.shape[0]
    res, drn = two_t[0:share], two_t[share : 2 * share]
    total = jnp.sum(arrived[...], axis=0)
    scalars = total[:, rank : rank + 2]
    res_res, curvature = scalars[0:share, 0:1], scalars[0:share, 1:2]
    img_img, res_img = scalars[share : 2 * share, 0:1], scalars[share : 2 * share, 1:2]
    alpha = prior[...] / curvature
    projected = total[0:share, 0:rank] - alpha * total[share : 2 * share, 0:rank]
    coeffs = dot(projected, inverse[...])
    coeffs = coeffs + dot(projected - dot(coeffs, gram[...]), inverse[...])
    norm = res_res - 2.0 * alpha * res_img + alpha * alpha * img_img
    product = norm - jnp.sum(projected * coeffs, axis=1, keepdims=True)
    new_res = res - alpha * image[...]
    padded = jnp.concatenate([coeffs, jnp.zeros((8 - share, rank), F32)], axis=0)
    precond = (new_res - stacked(padded, basis_3, NN)[0:share]) * (1.0 / noise_row[...])
    new_drn = precond + product / prior[...] * drn
    pieces = out.shape[0]
    own = new_res.shape[1] // pieces
    spare = jnp.zeros((share, 128 - 2 * own - 2), F32)
    for c in range(pieces):
        at = slice(c * own, (c + 1) * own)
        out[c] = jnp.concatenate([new_res[:, at], new_drn[:, at], alpha, product, spare], axis=1)


def finish_kernel(arrived, solution, direction, new_solution, new_residual, new_direction, new_product):
    own = solution.shape[0]
    t = arrived[...].T
    new_residual[...] = t[0:own]
    new_direction[...] = t[own : 2 * own]
    new_solution[...] = solution[...] + t[2 * own : 2 * own + 1] * direction[...]
    new_product[...] = t[2 * own + 1 : 2 * own + 2]


def exchange(pieces, axes):
    return lax.all_to_all(pieces, axes, split_axis=0, concat_axis=0, tiled=True)


def per_device(
    points,
    source_ids,
    source_shift,
    noise_level,
    weight_in,
    bias_in,
    weight_out,
    inverse_scale,
    frequency,
    phase_shift,
    solution,
    residual,
    direction,
    prior_product,
):
    row, col = lax.axis_size(ROW), lax.axis_size(COL)
    own, columns = direction.shape
    rank = frequency.shape[1]
    groups = own // 8
    share = columns // col
    count = own * col
    to_row, to_col, waves = call(
        features_kernel,
        (shape(own + 16, 128), shape(col, 8, 256), shape(rank + 16, 256, dtype=BF16)),
        points,
        source_ids.reshape(1, own),
        source_shift,
        noise_level.reshape(1, -1),
        weight_in,
        bias_in.reshape(1, -1),
        weight_out.T,
        inverse_scale.reshape(1, -1),
        frequency,
        phase_shift.reshape(1, -1),
        residual,
        direction,
        prior_product.reshape(1, -1),
        far=range(13),
        sent=(1,),
    )
    from_col = exchange(to_col, COL)
    from_row = lax.all_gather(to_row, ROW, axis=0, tiled=False)
    piece = 3 * rank // 2 // row
    i_side, two_t, noise_row, prior, basis_3, capacity = call(
        basis_kernel,
        (
            shape(count, 256, dtype=BF16),
            shape(2 * share, count),
            shape(1, count),
            shape(share, 1),
            shape(3, rank, count, dtype=BF16),
            shape(row, piece, rank // 2),
        ),
        from_col,
        waves,
        flops=6_000_000_000,
        sent=(0, 5),
        scratch=[pltpu.VMEM((col, groups, 8, 128), F32)],
    )
    parts = exchange(capacity, ROW)
    products = call(
        products_kernel,
        shape(col, share, count),
        from_row,
        i_side,
        flops=6_000_000_000,
        sent=(0,),
        scratch=[pltpu.VMEM((row, groups, 8, 128), F32)],
    )
    products = exchange(products, COL)
    own_rows = call(whole_kernel, shape(piece, rank // 2), parts)
    blocks = lax.all_gather(own_rows, ROW, axis=0, tiled=True)
    image, sums = call(
        sums_kernel,
        (shape(share, count), shape(row, 2 * share, rank + 128)),
        products,
        two_t,
        noise_row,
        basis_3,
        sent=(1,),
    )
    sums = exchange(sums, ROW)
    inverse, gram = call(
        inverse_kernel,
        (shape(rank, rank), shape(rank, rank)),
        blocks,
        flops=12_000_000_000,
    )
    results = call(
        solve_kernel,
        shape(col, share, 128),
        sums,
        prior,
        inverse,
        gram,
        two_t,
        noise_row,
        basis_3,
        image,
    )
    results = exchange(results, COL)
    new_solution, new_residual, new_direction, new_product = call(
        finish_kernel,
        (shape(own, columns), shape(own, columns), shape(own, columns), shape(1, columns)),
        results.reshape(columns, 128),
        solution,
        direction,
        sent=(0, 1, 2),
    )
    return new_solution, new_residual, new_direction, new_product.reshape(columns)


def solution(mesh):
    row, col = mesh.devices.shape
    split = Mesh(mesh.devices.reshape(row // 2, 2, col // 8, 8), ROW_COL)
    lines = P(ROW_COL, None)
    placed = (lines, P(ROW_COL)) + (P(),) * 8 + (lines, lines, lines, P())
    return jax.shard_map(
        per_device,
        mesh=split,
        in_specs=placed,
        out_specs=(lines, lines, lines, P()),
        check_vma=False,
    )
```

```python
import math

import jax
import jax.numpy as jnp
from jax import lax
from jax.experimental import pallas as pl
from jax.experimental.pallas import tpu as pltpu
from jax.sharding import Mesh
from jax.sharding import PartitionSpec as P

ROW = ("y", "core")
COL = ("x", "z")
ROW_COL = ROW + COL
HIGH = lax.Precision.HIGHEST
F32 = jnp.float32
BF16 = jnp.bfloat16
NN = (((1,), (0,)), ((), ()))
NT = (((1,), (1,)), ((), ()))

def call(kernel, outs, *args, flops=1_000_000, scratch=(), far=(), sent=()):
    vmem, hbm = pl.BlockSpec(memory_space=pltpu.VMEM), pl.BlockSpec(memory_space=pltpu.HBM)
    flat = outs if isinstance(outs, tuple) else (outs,)
    far, sent = list(far), list(sent)
    copied = [args[i] for i in far] + [flat[i] for i in sent]

    def body(*refs):
        ins, res = list(refs[: len(args)]), list(refs[len(args) : len(args) + len(flat)])
        rest = refs[len(args) + len(flat) :]
        rest, held = rest[: len(scratch)], rest[len(scratch) :]
        if not copied:
            return kernel(*ins, *res, *rest)
        held, done = held[:-1], held[-1]
        into = [pltpu.make_async_copy(ins[i], held[n], done.at[n]) for n, i in enumerate(far)]
        for copy in into:
            copy.start()
        for n, i in enumerate(far):
            ins[i] = held[n]
        out = []
        for n, i in enumerate(sent, len(far)):
            out.append(pltpu.make_async_copy(held[n], res[i], done.at[n]))
            res[i] = held[n]
        for copy in into:
            copy.wait()
        kernel(*ins, *res, *rest)
        for copy in out:
            copy.start()
        for copy in out:
            copy.wait()

    extra = [pltpu.VMEM(a.shape, a.dtype) for a in copied]
    if copied:
        extra.append(pltpu.SemaphoreType.DMA((len(copied),)))
    args = [pltpu.with_memory_space_constraint(a, pltpu.HBM) if i in far else a for i, a in enumerate(args)]
    results = pl.pallas_call(
        body,
        out_shape=flat,
        in_specs=[hbm if i in far else vmem for i in range(len(args))],
        out_specs=tuple(hbm if i in sent else vmem for i in range(len(flat))),
        scratch_shapes=list(scratch) + extra,
        compiler_params=pltpu.CompilerParams(vmem_limit_bytes=16 * 2**20),
        cost_estimate=pl.CostEstimate(flops=flops, bytes_accessed=100_000, transcendentals=0),
    )(*args)
    return results if isinstance(outs, tuple) else results[0]


def shape(*dims, dtype=F32):
    return jax.ShapeDtypeStruct(dims, dtype)


def dot(a, b, dims=NN):
    return lax.dot_general(a, b, dims, precision=HIGH, preferred_element_type=F32)


def dot16(a, b, dims=NN):
    return lax.dot_general(a, b, dims, preferred_element_type=F32)


def three(x):
    h = x.astype(BF16).astype(F32)
    m = (x - h).astype(BF16).astype(F32)
    return h, m, (x - h - m).astype(BF16).astype(F32)


def stacked(x, b, dims):
    b3 = [part.astype(BF16) for part in three(b)]
    h, m, l = three(x)
    none = jnp.zeros_like(x)
    by_h = dot16(jnp.concatenate([h, m, l, none], axis=0).astype(BF16), b3[0], dims)
    by_m = dot16(jnp.concatenate([h, m], axis=0).astype(BF16), b3[1], dims)
    by_l = dot16(jnp.concatenate([h, none], axis=0).astype(BF16), b3[2], dims)
    return by_h[0:8] + (by_h[8:16] + by_m[0:8] + (by_h[16:24] + by_m[8:16] + by_l[0:8]))


def shifted_by(x, lanes):
    return pltpu.roll(x, lanes, 1)


def left_side(x):
    h, m, l = three(x)
    one = h + shifted_by(h, 42) + shifted_by(m, 84)
    two = h + shifted_by(l, 42) + shifted_by(m, 84)
    return jnp.concatenate([one, two], axis=1).astype(BF16)


def right_side(x):
    h, m, l = three(x)
    one = h + shifted_by(m, 42) + shifted_by(h, 84)
    two = l + shifted_by(h, 42) + shifted_by(m, 84)
    return jnp.concatenate([one, two], axis=1).astype(BF16)


def cosine(turns, scale):
    t = 0.25 - jnp.abs(turns - jnp.floor(turns + 0.5))
    s = t * t
    p = 0.0
    for k in range(5, -1, -1):
        c = (-1) ** k * scale * (2.0 * math.pi) ** (2 * k + 1) / math.factorial(2 * k + 1)
        p = p * s + c
    return p * t


def lane_of(rows, lanes=128):
    return lax.broadcasted_iota(jnp.int32, (rows, lanes), 1)


def features_kernel(
    points, ids, shift, level, w_in, b_in, w_out_t, inv, freq, phase, res, drn, prior, to_row, to_col, waves
):
    own = points.shape[0]
    groups = own // 8
    sources = shift.shape[0]
    hot_t = (lax.broadcasted_iota(jnp.int32, (sources, own), 0) == ids[...]).astype(F32)
    hot = hot_t.T
    shifted = points[...] + dot(hot, shift[...])
    hidden = jnp.tanh(dot(shifted, w_in[...]) + b_in[...])
    f = dot(hidden, w_out_t[...], NT) * inv[...]
    n = -0.5 * jnp.sum(f * f, axis=1, keepdims=True)
    noise = dot(hot, jnp.broadcast_to(level[...], (8, sources)), NT)[:, 0:1]
    first = jnp.concatenate([f[8 * g : 8 * g + 8] for g in range(4)], axis=1)
    second = jnp.concatenate(
        [f[8 * g : 8 * g + 8] for g in range(4, groups)]
        + [jnp.zeros((8, own), F32)]
        + [x[8 * g : 8 * g + 8] for g in range(groups) for x in (n, noise)]
        + [jnp.zeros((8, 128 - 32 - own - 2 * groups), F32)],
        axis=1,
    )
    to_row[0:own, :] = drn[...]
    to_row[own : own + 8, :] = first
    to_row[own + 8 : own + 16, :] = second
    col = to_col.shape[0]
    share = res.shape[1] // col

    def turned(x):
        low, high = jnp.zeros((32, 128), F32), jnp.zeros((128 - 32 - own, 128), F32)
        return jnp.concatenate([low, x, high], axis=0).T

    prior_t = jnp.broadcast_to(prior[...], (128, 128)).T
    res_t = jnp.where(lane_of(128) == 32 + own + 2 * groups, prior_t, turned(res[...]))
    drn_t = turned(drn[...])
    spare = [jnp.zeros((8 - 2 * share, 128), F32)] if share < 4 else []
    for c in range(col):
        at = slice(c * share, (c + 1) * share)
        to_col[c, :, 0:128] = first
        to_col[c, :, 128:256] = second + jnp.concatenate([res_t[at], drn_t[at]] + spare, axis=0)
    feat = freq.shape[0]
    rank = freq.shape[1]
    table = jnp.concatenate(
        [
            freq[...],
            jnp.zeros((2, rank), F32),
            phase[...],
            jnp.zeros((128 - feat - 3, rank), F32),
        ],
        axis=0,
    ).T
    pick = jnp.where(lane_of(waves.shape[0] - rank) == feat + 1, 1.0, 0.0)
    waves[...] = right_side(jnp.concatenate([table * (0.5 / math.pi), pick], axis=0))


def unpacked(first, second, x):
    groups = x.shape[1]
    own = groups * 8
    for g in range(groups):
        source = first[:, :, 32 * g : 32 * g + 32] if g < 4 else second[:, :, 32 * g - 128 : 32 * g - 96]
        x[:, g, :, 0:32] = source
        at = 32 + own + 2 * g
        x[:, g, :, 32:34] = second[:, :, at : at + 2]
    return x[...].reshape(x.shape[0] * own, 128)


def row_side(arrived, x):
    values = unpacked(arrived[:, :, 0:128], arrived[:, :, 128:256], x)
    lane = lane_of(values.shape[0])
    return left_side(jnp.where(lane < 34, values, jnp.where(lane == 34, 1.0, 0.0)))


def basis_kernel(arrived, waves, noise_row, prior, basis_t, capacity, x):
    groups = x.shape[1]
    own = groups * 8
    share = prior.shape[0]
    side = row_side(arrived, x)
    at = 160 + own + 2 * groups
    prior[...] = arrived[0, 0:share, at : at + 1]
    rank = basis_t.shape[0]
    half = rank // 2
    turned = dot16(waves[...], side, NT)
    noise = turned[rank : rank + 1]
    noise_row[...] = noise
    basis = cosine(turned[0:rank], math.sqrt(2.0 / rank))
    basis_t[...] = basis
    weighted = basis * (1.0 / noise)
    full = dot(weighted, basis, NT)
    blocks = jnp.concatenate([full[:, 0:half], full[half:, half:]], axis=0)
    capacity[...] = blocks.reshape(capacity.shape)


def products_kernel(arrived, from_col, out, two_t, x, x_col):
    pieces, groups = x.shape[0], x.shape[1]
    own = groups * 8
    col, share = out.shape[0], out.shape[1]
    values = unpacked(arrived[:, own : own + 8, :], arrived[:, own + 8 : own + 16, :], x)
    lane = lane_of(values.shape[0])
    norm = jnp.where(lane == 32, values, 0.0)
    values = jnp.where(lane < 32, values, jnp.where(lane == 32, 1.0, 0.0)) + shifted_by(norm, 2)
    j_side = right_side(values)
    d_t = arrived[:, 0:own, :].reshape(pieces * own, 128).T
    high = d_t.astype(BF16)
    low = (d_t - high.astype(F32)).astype(BF16)
    both = jnp.concatenate([high, low], axis=0)
    i_side = row_side(from_col, x_col)
    for c in range(col):
        two_t[:, own * c : own * (c + 1)] = from_col[c, 0 : 2 * share, 160 : 160 + own]
    count = i_side.shape[0]
    step = 256
    for i in range(count // step):
        k = jnp.exp(dot16(j_side, i_side[i * step : (i + 1) * step, :], NT))
        k_high = k.astype(BF16)
        k_low = (k - k_high.astype(F32)).astype(BF16)
        pair = dot16(both, k_high)
        total = pair[0:128] + (pair[128:256] + dot16(high, k_low))
        for c in range(col):
            out[c, :, i * step : (i + 1) * step] = total[share * c : share * (c + 1)]


def whole_kernel(parts, out):
    out[...] = jnp.sum(parts[...], axis=0)


def eliminated(p, base, lane, one_lane, sub):
    size, rank = p.shape
    for t in range(0, size, 4):
        j = base + t
        c = [jnp.broadcast_to(p[:, j + i : j + i + 1], (size, rank)) for i in range(4)]
        s = [[c[i][t + q : t + q + 1] for q in range(4)] for i in range(4)]
        inside = (one_lane >= j) & (one_lane < j + 4)
        r = [
            jnp.where(inside, jnp.where(one_lane == j + i, 1.0, 0.0), p[t + i : t + i + 1])
            for i in range(4)
        ]
        inv = 1.0 / (s[0][0] * s[1][1] - s[0][1] * s[0][1])
        a0, a1, a2 = s[1][1] * inv, -s[0][1] * inv, s[0][0] * inv
        g02, g03 = a0 * s[2][0] + a1 * s[2][1], a0 * s[3][0] + a1 * s[3][1]
        g12, g13 = a1 * s[2][0] + a2 * s[2][1], a1 * s[3][0] + a2 * s[3][1]
        e = s[2][2] - s[2][0] * g02 - s[2][1] * g12
        f = s[3][2] - s[2][0] * g03 - s[2][1] * g13
        h = s[3][3] - s[3][0] * g03 - s[3][1] * g13
        inv = 1.0 / (e * h - f * f)
        e, f, h = h * inv, -f * inv, e * inv
        v2 = r[2] - g02 * r[0] - g12 * r[1]
        v3 = r[3] - g03 * r[0] - g13 * r[1]
        u2 = e * v2 + f * v3
        u3 = f * v2 + h * v3
        u0 = a0 * r[0] + a1 * r[1] - g02 * u2 - g03 * u3
        u1 = a1 * r[0] + a2 * r[1] - g12 * u2 - g13 * u3
        here = (sub >= t) & (sub < t + 4)
        p = jnp.where(((lane < j) | (lane >= j + 4)) & ~here, p, 0.0)
        for i, u in enumerate((u0, u1, u2, u3)):
            p = p - jnp.where(here, jnp.where(sub == t + i, -1.0, 0.0), c[i]) * u
    return p


def inverse_kernel(blocks, out, gram):
    rank = out.shape[0]
    size = 32
    rows = lax.broadcasted_iota(jnp.int32, (rank, rank), 0)
    cols = lax.broadcasted_iota(jnp.int32, (rank, rank), 1)
    half = rank // 2
    one, two, three_ = blocks[0:half], blocks[half:rank], blocks[rank : rank + half]
    m = jnp.concatenate(
        [jnp.concatenate([one, two.T], axis=1), jnp.concatenate([two, three_], axis=1)], axis=0
    )
    m = m + jnp.where(rows == cols, 1.0, 0.0)
    gram[...] = m
    count = rank // size
    panels = [m[i * size : (i + 1) * size] for i in range(count)]
    lane, one_lane = lane_of(size, rank), lane_of(1, rank)
    sub = lax.broadcasted_iota(jnp.int32, (size, rank), 0)
    for k in range(count):
        base = k * size
        p = eliminated(panels[k], base, lane, one_lane, sub)
        panels[k] = p

        def updated(x):
            at = lane_of(x.shape[0], rank)
            inside = (at >= base) & (at < base + size)
            return jnp.where(inside, 0.0, x) - dot(x[:, base : base + size], p)

        others = [i for i in range(count) if i != k]
        if k + 1 < count:
            panels[k + 1] = updated(panels[k + 1])
            others.remove(k + 1)
        rest = updated(jnp.concatenate([panels[i] for i in others], axis=0))
        for w, i in enumerate(others):
            panels[i] = rest[w * size : (w + 1) * size]
    for i in range(count):
        out[i * size : (i + 1) * size] = panels[i]


def sums_kernel(arrived, two_t, noise_row, basis_t, image, out):
    share = image.shape[0]
    res, drn = two_t[0:share], two_t[share : 2 * share]
    noise = noise_row[...]
    value = jnp.sum(arrived[...], axis=0) + noise * drn
    image[...] = value
    stack = jnp.concatenate([res, value], axis=0)
    scaled = stack * (1.0 / noise)
    proj = stacked(scaled, basis_t[...], NT)
    over = scaled[share:]
    left = jnp.concatenate(
        [jnp.sum(res * scaled[0:share], axis=1, keepdims=True), jnp.sum(value * over, axis=1, keepdims=True)],
        axis=0,
    )
    right = jnp.concatenate(
        [jnp.sum(drn * value, axis=1, keepdims=True), jnp.sum(res * over, axis=1, keepdims=True)],
        axis=0,
    )
    lane = lane_of(2 * share)
    scalars = jnp.where(lane == 0, left, jnp.where(lane == 1, right, 0.0))
    rank = proj.shape[1]
    for r in range(out.shape[0]):
        out[r, :, 0:rank] = proj
        out[r, :, rank : rank + 128] = scalars


def solve_kernel(arrived, prior, inverse, gram, two_t, noise_row, basis_t, image, out):
    share = image.shape[0]
    rank = gram.shape[0]
    res, drn = two_t[0:share], two_t[share : 2 * share]
    total = jnp.sum(arrived[...], axis=0)
    scalars = total[:, rank : rank + 2]
    res_res, curvature = scalars[0:share, 0:1], scalars[0:share, 1:2]
    img_img, res_img = scalars[share : 2 * share, 0:1], scalars[share : 2 * share, 1:2]
    alpha = prior[...] / curvature
    projected = total[0:share, 0:rank] - alpha * total[share : 2 * share, 0:rank]
    coeffs = dot(projected, inverse[...])
    coeffs = coeffs + dot(projected - dot(coeffs, gram[...]), inverse[...])
    norm = res_res - 2.0 * alpha * res_img + alpha * alpha * img_img
    product = norm - jnp.sum(projected * coeffs, axis=1, keepdims=True)
    new_res = res - alpha * image[...]
    padded = jnp.concatenate([coeffs, jnp.zeros((8 - share, rank), F32)], axis=0)
    precond = (new_res - stacked(padded, basis_t[...], NN)[0:share]) * (1.0 / noise_row[...])
    new_drn = precond + product / prior[...] * drn
    pieces = out.shape[0]
    own = new_res.shape[1] // pieces
    spare = jnp.zeros((share, 128 - 2 * own - 2), F32)
    for c in range(pieces):
        at = slice(c * own, (c + 1) * own)
        out[c] = jnp.concatenate([new_res[:, at], new_drn[:, at], alpha, product, spare], axis=1)


def finish_kernel(arrived, solution, direction, new_solution, new_residual, new_direction, new_product):
    own = solution.shape[0]
    t = arrived[...].T
    new_residual[...] = t[0:own]
    new_direction[...] = t[own : 2 * own]
    new_solution[...] = solution[...] + t[2 * own : 2 * own + 1] * direction[...]
    new_product[...] = t[2 * own + 1 : 2 * own + 2]


def exchange(pieces, axes):
    return lax.all_to_all(pieces, axes, split_axis=0, concat_axis=0, tiled=True)


def per_device(
    points,
    source_ids,
    source_shift,
    noise_level,
    weight_in,
    bias_in,
    weight_out,
    inverse_scale,
    frequency,
    phase_shift,
    solution,
    residual,
    direction,
    prior_product,
):
    row, col = lax.axis_size(ROW), lax.axis_size(COL)
    own, columns = direction.shape
    rank = frequency.shape[1]
    groups = own // 8
    share = columns // col
    count = own * col
    to_row, to_col, waves = call(
        features_kernel,
        (shape(own + 16, 128), shape(col, 8, 256), shape(rank + 16, 256, dtype=BF16)),
        points,
        source_ids.reshape(1, own),
        source_shift,
        noise_level.reshape(1, -1),
        weight_in,
        bias_in.reshape(1, -1),
        weight_out.T,
        inverse_scale.reshape(1, -1),
        frequency,
        phase_shift.reshape(1, -1),
        residual,
        direction,
        prior_product.reshape(1, -1),
        far=range(13),
        sent=(1,),
    )
    from_col = exchange(to_col, COL)
    from_row = lax.all_gather(to_row, ROW, axis=0, tiled=False)
    piece = 3 * rank // 2 // row
    noise_row, prior, basis_t, capacity = call(
        basis_kernel,
        (shape(1, count), shape(share, 1), shape(rank, count), shape(row, piece, rank // 2)),
        from_col,
        waves,
        flops=6_000_000_000,
        sent=(3,),
        scratch=[pltpu.VMEM((col, groups, 8, 128), F32)],
    )
    parts = exchange(capacity, ROW)
    products, two_t = call(
        products_kernel,
        (shape(col, share, count), shape(2 * share, count)),
        from_row,
        from_col,
        flops=6_000_000_000,
        sent=(0,),
        scratch=[
            pltpu.VMEM((row, groups, 8, 128), F32),
            pltpu.VMEM((col, groups, 8, 128), F32),
        ],
    )
    products = exchange(products, COL)
    own_rows = call(whole_kernel, shape(piece, rank // 2), parts)
    blocks = lax.all_gather(own_rows, ROW, axis=0, tiled=True)
    image, sums = call(
        sums_kernel,
        (shape(share, count), shape(row, 2 * share, rank + 128)),
        products,
        two_t,
        noise_row,
        basis_t,
        sent=(1,),
    )
    sums = exchange(sums, ROW)
    inverse, gram = call(
        inverse_kernel,
        (shape(rank, rank), shape(rank, rank)),
        blocks,
        flops=12_000_000_000,
    )
    results = call(
        solve_kernel,
        shape(col, share, 128),
        sums,
        prior,
        inverse,
        gram,
        two_t,
        noise_row,
        basis_t,
        image,
    )
    results = exchange(results, COL)
    new_solution, new_residual, new_direction, new_product = call(
        finish_kernel,
        (shape(own, columns), shape(own, columns), shape(own, columns), shape(1, columns)),
        results.reshape(columns, 128),
        solution,
        direction,
        sent=(0, 1, 2),
    )
    return new_solution, new_residual, new_direction, new_product.reshape(columns)


def solution(mesh):
    row, col = mesh.devices.shape
    split = Mesh(mesh.devices.reshape(row // 2, 2, col // 8, 8), ROW_COL)
    lines = P(ROW_COL, None)
    placed = (lines, P(ROW_COL)) + (P(),) * 8 + (lines, lines, lines, P())
    return jax.shard_map(
        per_device,
        mesh=split,
        in_specs=placed,
        out_specs=(lines, lines, lines, P()),
        check_vma=False,
    )
```

```python
import math

import jax
import jax.numpy as jnp
from jax import lax
from jax.experimental import pallas as pl
from jax.experimental.pallas import tpu as pltpu
from jax.sharding import Mesh
from jax.sharding import PartitionSpec as P

ROW = ("y", "core")
COL = ("x", "z")
ROW_COL = ROW + COL
HIGH = lax.Precision.HIGHEST
F32 = jnp.float32
BF16 = jnp.bfloat16
NN = (((1,), (0,)), ((), ()))
NT = (((1,), (1,)), ((), ()))

def call(kernel, outs, *args, flops=1_000_000, scratch=(), far=(), sent=()):
    vmem, hbm = pl.BlockSpec(memory_space=pltpu.VMEM), pl.BlockSpec(memory_space=pltpu.HBM)
    flat = outs if isinstance(outs, tuple) else (outs,)
    far, sent = list(far), list(sent)
    copied = [args[i] for i in far] + [flat[i] for i in sent]

    def body(*refs):
        ins, res = list(refs[: len(args)]), list(refs[len(args) : len(args) + len(flat)])
        rest = refs[len(args) + len(flat) :]
        rest, held = rest[: len(scratch)], rest[len(scratch) :]
        if not copied:
            return kernel(*ins, *res, *rest)
        held, done = held[:-1], held[-1]
        into = [pltpu.make_async_copy(ins[i], held[n], done.at[n]) for n, i in enumerate(far)]
        for copy in into:
            copy.start()
        for n, i in enumerate(far):
            ins[i] = held[n]
        out = []
        for n, i in enumerate(sent, len(far)):
            out.append(pltpu.make_async_copy(held[n], res[i], done.at[n]))
            res[i] = held[n]
        for copy in into:
            copy.wait()
        kernel(*ins, *res, *rest)
        for copy in out:
            copy.start()
        for copy in out:
            copy.wait()

    extra = [pltpu.VMEM(a.shape, a.dtype) for a in copied]
    if copied:
        extra.append(pltpu.SemaphoreType.DMA((len(copied),)))
    args = [pltpu.with_memory_space_constraint(a, pltpu.HBM) if i in far else a for i, a in enumerate(args)]
    results = pl.pallas_call(
        body,
        out_shape=flat,
        in_specs=[hbm if i in far else vmem for i in range(len(args))],
        out_specs=tuple(hbm if i in sent else vmem for i in range(len(flat))),
        scratch_shapes=list(scratch) + extra,
        compiler_params=pltpu.CompilerParams(vmem_limit_bytes=16 * 2**20),
        cost_estimate=pl.CostEstimate(flops=flops, bytes_accessed=100_000, transcendentals=0),
    )(*args)
    return results if isinstance(outs, tuple) else results[0]


def shape(*dims, dtype=F32):
    return jax.ShapeDtypeStruct(dims, dtype)


def dot(a, b, dims=NN):
    return lax.dot_general(a, b, dims, precision=HIGH, preferred_element_type=F32)


def dot16(a, b, dims=NN):
    return lax.dot_general(a, b, dims, preferred_element_type=F32)


def three(x):
    h = x.astype(BF16).astype(F32)
    m = (x - h).astype(BF16).astype(F32)
    return h, m, (x - h - m).astype(BF16).astype(F32)


def stacked(x, b, dims):
    b3 = [part.astype(BF16) for part in three(b)]
    h, m, l = three(x)
    none = jnp.zeros_like(x)
    by_h = dot16(jnp.concatenate([h, m, l, none], axis=0).astype(BF16), b3[0], dims)
    by_m = dot16(jnp.concatenate([h, m], axis=0).astype(BF16), b3[1], dims)
    by_l = dot16(jnp.concatenate([h, none], axis=0).astype(BF16), b3[2], dims)
    return by_h[0:8] + (by_h[8:16] + by_m[0:8] + (by_h[16:24] + by_m[8:16] + by_l[0:8]))


def shifted_by(x, lanes):
    return pltpu.roll(x, lanes, 1)


def left_side(x):
    h, m, l = three(x)
    one = h + shifted_by(h, 42) + shifted_by(m, 84)
    two = h + shifted_by(l, 42) + shifted_by(m, 84)
    return jnp.concatenate([one, two], axis=1).astype(BF16)


def right_side(x):
    h, m, l = three(x)
    one = h + shifted_by(m, 42) + shifted_by(h, 84)
    two = l + shifted_by(h, 42) + shifted_by(m, 84)
    return jnp.concatenate([one, two], axis=1).astype(BF16)


def cosine(turns, scale):
    t = 0.25 - jnp.abs(turns - jnp.floor(turns + 0.5))
    s = t * t
    p = 0.0
    for k in range(5, -1, -1):
        c = (-1) ** k * scale * (2.0 * math.pi) ** (2 * k + 1) / math.factorial(2 * k + 1)
        p = p * s + c
    return p * t


def lane_of(rows, lanes=128):
    return lax.broadcasted_iota(jnp.int32, (rows, lanes), 1)


def features_kernel(
    points, ids, shift, level, w_in, b_in, w_out_t, inv, freq, phase, res, drn, prior, to_row, to_col, waves
):
    own = points.shape[0]
    groups = own // 8
    sources = shift.shape[0]
    hot_t = (lax.broadcasted_iota(jnp.int32, (sources, own), 0) == ids[...]).astype(F32)
    hot = hot_t.T
    shifted = points[...] + dot(hot, shift[...])
    hidden = jnp.tanh(dot(shifted, w_in[...]) + b_in[...])
    f = dot(hidden, w_out_t[...], NT) * inv[...]
    n = -0.5 * jnp.sum(f * f, axis=1, keepdims=True)
    noise = dot(hot, jnp.broadcast_to(level[...], (8, sources)), NT)[:, 0:1]
    first = jnp.concatenate([f[8 * g : 8 * g + 8] for g in range(4)], axis=1)
    second = jnp.concatenate(
        [f[8 * g : 8 * g + 8] for g in range(4, groups)]
        + [jnp.zeros((8, own), F32)]
        + [x[8 * g : 8 * g + 8] for g in range(groups) for x in (n, noise)]
        + [jnp.zeros((8, 128 - 32 - own - 2 * groups), F32)],
        axis=1,
    )
    to_row[0:own, :] = drn[...]
    to_row[own : own + 8, :] = first
    to_row[own + 8 : own + 16, :] = second
    col = to_col.shape[0]
    share = res.shape[1] // col

    def turned(x):
        low, high = jnp.zeros((32, 128), F32), jnp.zeros((128 - 32 - own, 128), F32)
        return jnp.concatenate([low, x, high], axis=0).T

    prior_t = jnp.broadcast_to(prior[...], (128, 128)).T
    res_t = jnp.where(lane_of(128) == 32 + own + 2 * groups, prior_t, turned(res[...]))
    drn_t = turned(drn[...])
    spare = [jnp.zeros((8 - 2 * share, 128), F32)] if share < 4 else []
    for c in range(col):
        at = slice(c * share, (c + 1) * share)
        to_col[c, :, 0:128] = first
        to_col[c, :, 128:256] = second + jnp.concatenate([res_t[at], drn_t[at]] + spare, axis=0)
    feat = freq.shape[0]
    rank = freq.shape[1]
    table = jnp.concatenate(
        [
            freq[...],
            jnp.zeros((2, rank), F32),
            phase[...],
            jnp.zeros((128 - feat - 3, rank), F32),
        ],
        axis=0,
    ).T
    pick = jnp.where(lane_of(waves.shape[0] - rank) == feat + 1, 1.0, 0.0)
    waves[...] = right_side(jnp.concatenate([table * (0.5 / math.pi), pick], axis=0))


def unpacked(first, second, x):
    groups = x.shape[1]
    own = groups * 8
    for g in range(groups):
        source = first[:, :, 32 * g : 32 * g + 32] if g < 4 else second[:, :, 32 * g - 128 : 32 * g - 96]
        x[:, g, :, 0:32] = source
        at = 32 + own + 2 * g
        x[:, g, :, 32:34] = second[:, :, at : at + 2]
    return x[...].reshape(x.shape[0] * own, 128)


def row_side(arrived, x):
    values = unpacked(arrived[:, :, 0:128], arrived[:, :, 128:256], x)
    lane = lane_of(values.shape[0])
    return left_side(jnp.where(lane < 34, values, jnp.where(lane == 34, 1.0, 0.0)))


def basis_kernel(arrived, waves, noise_row, prior, basis_t, capacity, x):
    groups = x.shape[1]
    own = groups * 8
    share = prior.shape[0]
    side = row_side(arrived, x)
    at = 160 + own + 2 * groups
    prior[...] = arrived[0, 0:share, at : at + 1]
    rank = basis_t.shape[0]
    half = rank // 2
    turned = dot16(waves[...], side, NT)
    noise = turned[rank : rank + 1]
    noise_row[...] = noise
    basis = cosine(turned[0:rank], math.sqrt(2.0 / rank))
    basis_t[...] = basis
    weighted = basis * (1.0 / noise)
    full = dot(weighted, basis, NT)
    blocks = jnp.concatenate([full[:, 0:half], full[half:, half:]], axis=0)
    capacity[...] = blocks.reshape(capacity.shape)


def products_kernel(arrived, from_col, out, two_t, x, x_col):
    pieces, groups = x.shape[0], x.shape[1]
    own = groups * 8
    col, share = out.shape[0], out.shape[1]
    values = unpacked(arrived[:, own : own + 8, :], arrived[:, own + 8 : own + 16, :], x)
    lane = lane_of(values.shape[0])
    norm = jnp.where(lane == 32, values, 0.0)
    values = jnp.where(lane < 32, values, jnp.where(lane == 32, 1.0, 0.0)) + shifted_by(norm, 2)
    j_side = right_side(values)
    d_t = arrived[:, 0:own, :].reshape(pieces * own, 128).T
    high = d_t.astype(BF16)
    low = (d_t - high.astype(F32)).astype(BF16)
    both = jnp.concatenate([high, low], axis=0)
    i_side = row_side(from_col, x_col)
    for c in range(col):
        two_t[:, own * c : own * (c + 1)] = from_col[c, 0 : 2 * share, 160 : 160 + own]
    count = i_side.shape[0]
    step = 256
    for i in range(count // step):
        k = jnp.exp(dot16(j_side, i_side[i * step : (i + 1) * step, :], NT))
        k_high = k.astype(BF16)
        k_low = (k - k_high.astype(F32)).astype(BF16)
        pair = dot16(both, k_high)
        total = pair[0:128] + (pair[128:256] + dot16(high, k_low))
        for c in range(col):
            out[c, :, i * step : (i + 1) * step] = total[share * c : share * (c + 1)]


def whole_kernel(parts, out):
    out[...] = jnp.sum(parts[...], axis=0)


def eliminated(p, base, lane, one_lane, sub):
    size, rank = p.shape
    for t in range(0, size, 4):
        j = base + t
        c = [jnp.broadcast_to(p[:, j + i : j + i + 1], (size, rank)) for i in range(4)]
        s = [[c[i][t + q : t + q + 1] for q in range(4)] for i in range(4)]
        inside = (one_lane >= j) & (one_lane < j + 4)
        r = [
            jnp.where(inside, jnp.where(one_lane == j + i, 1.0, 0.0), p[t + i : t + i + 1])
            for i in range(4)
        ]
        inv = 1.0 / (s[0][0] * s[1][1] - s[0][1] * s[0][1])
        a0, a1, a2 = s[1][1] * inv, -s[0][1] * inv, s[0][0] * inv
        g02, g03 = a0 * s[2][0] + a1 * s[2][1], a0 * s[3][0] + a1 * s[3][1]
        g12, g13 = a1 * s[2][0] + a2 * s[2][1], a1 * s[3][0] + a2 * s[3][1]
        e = s[2][2] - s[2][0] * g02 - s[2][1] * g12
        f = s[3][2] - s[2][0] * g03 - s[2][1] * g13
        h = s[3][3] - s[3][0] * g03 - s[3][1] * g13
        inv = 1.0 / (e * h - f * f)
        e, f, h = h * inv, -f * inv, e * inv
        v2 = r[2] - g02 * r[0] - g12 * r[1]
        v3 = r[3] - g03 * r[0] - g13 * r[1]
        u2 = e * v2 + f * v3
        u3 = f * v2 + h * v3
        u0 = a0 * r[0] + a1 * r[1] - g02 * u2 - g03 * u3
        u1 = a1 * r[0] + a2 * r[1] - g12 * u2 - g13 * u3
        here = (sub >= t) & (sub < t + 4)
        p = jnp.where(((lane < j) | (lane >= j + 4)) & ~here, p, 0.0)
        for i, u in enumerate((u0, u1, u2, u3)):
            p = p - jnp.where(here, jnp.where(sub == t + i, -1.0, 0.0), c[i]) * u
    return p


def eliminate(m, first, last):
    rank = m.shape[0]
    size = 32
    count = rank // size
    panels = [m[i * size : (i + 1) * size] for i in range(count)]
    lane, one_lane = lane_of(size, rank), lane_of(1, rank)
    sub = lax.broadcasted_iota(jnp.int32, (size, rank), 0)
    for k in range(first, last):
        base = k * size
        p = eliminated(panels[k], base, lane, one_lane, sub)
        panels[k] = p

        def updated(x):
            at = lane_of(x.shape[0], rank)
            inside = (at >= base) & (at < base + size)
            return jnp.where(inside, 0.0, x) - dot(x[:, base : base + size], p)

        others = [i for i in range(count) if i != k]
        if k + 1 < count:
            panels[k + 1] = updated(panels[k + 1])
            others.remove(k + 1)
        rest = updated(jnp.concatenate([panels[i] for i in others], axis=0))
        for w, i in enumerate(others):
            panels[i] = rest[w * size : (w + 1) * size]
    return panels


EARLY = 2


def early_kernel(blocks, out, gram):
    rank = out.shape[0]
    rows = lax.broadcasted_iota(jnp.int32, (rank, rank), 0)
    cols = lax.broadcasted_iota(jnp.int32, (rank, rank), 1)
    half = rank // 2
    one, two, three_ = blocks[0:half], blocks[half:rank], blocks[rank : rank + half]
    m = jnp.concatenate(
        [jnp.concatenate([one, two.T], axis=1), jnp.concatenate([two, three_], axis=1)], axis=0
    )
    m = m + jnp.where(rows == cols, 1.0, 0.0)
    gram[...] = m
    for i, panel in enumerate(eliminate(m, 0, EARLY)):
        out[i * 32 : (i + 1) * 32] = panel


def inverse_kernel(begun, out):
    for i, panel in enumerate(eliminate(begun[...], EARLY, out.shape[0] // 32)):
        out[i * 32 : (i + 1) * 32] = panel


def sums_kernel(arrived, two_t, noise_row, basis_t, image, out):
    share = image.shape[0]
    res, drn = two_t[0:share], two_t[share : 2 * share]
    noise = noise_row[...]
    value = jnp.sum(arrived[...], axis=0) + noise * drn
    image[...] = value
    stack = jnp.concatenate([res, value], axis=0)
    scaled = stack * (1.0 / noise)
    proj = stacked(scaled, basis_t[...], NT)
    over = scaled[share:]
    left = jnp.concatenate(
        [jnp.sum(res * scaled[0:share], axis=1, keepdims=True), jnp.sum(value * over, axis=1, keepdims=True)],
        axis=0,
    )
    right = jnp.concatenate(
        [jnp.sum(drn * value, axis=1, keepdims=True), jnp.sum(res * over, axis=1, keepdims=True)],
        axis=0,
    )
    lane = lane_of(2 * share)
    scalars = jnp.where(lane == 0, left, jnp.where(lane == 1, right, 0.0))
    rank = proj.shape[1]
    for r in range(out.shape[0]):
        out[r, :, 0:rank] = proj
        out[r, :, rank : rank + 128] = scalars


def solve_kernel(arrived, prior, inverse, gram, two_t, noise_row, basis_t, image, out):
    share = image.shape[0]
    rank = gram.shape[0]
    res, drn = two_t[0:share], two_t[share : 2 * share]
    total = jnp.sum(arrived[...], axis=0)
    scalars = total[:, rank : rank + 2]
    res_res, curvature = scalars[0:share, 0:1], scalars[0:share, 1:2]
    img_img, res_img = scalars[share : 2 * share, 0:1], scalars[share : 2 * share, 1:2]
    alpha = prior[...] / curvature
    projected = total[0:share, 0:rank] - alpha * total[share : 2 * share, 0:rank]
    coeffs = dot(projected, inverse[...])
    coeffs = coeffs + dot(projected - dot(coeffs, gram[...]), inverse[...])
    norm = res_res - 2.0 * alpha * res_img + alpha * alpha * img_img
    product = norm - jnp.sum(projected * coeffs, axis=1, keepdims=True)
    new_res = res - alpha * image[...]
    padded = jnp.concatenate([coeffs, jnp.zeros((8 - share, rank), F32)], axis=0)
    precond = (new_res - stacked(padded, basis_t[...], NN)[0:share]) * (1.0 / noise_row[...])
    new_drn = precond + product / prior[...] * drn
    pieces = out.shape[0]
    own = new_res.shape[1] // pieces
    spare = jnp.zeros((share, 128 - 2 * own - 2), F32)
    for c in range(pieces):
        at = slice(c * own, (c + 1) * own)
        out[c] = jnp.concatenate([new_res[:, at], new_drn[:, at], alpha, product, spare], axis=1)


def finish_kernel(arrived, solution, direction, new_solution, new_residual, new_direction, new_product):
    own = solution.shape[0]
    t = arrived[...].T
    new_residual[...] = t[0:own]
    new_direction[...] = t[own : 2 * own]
    new_solution[...] = solution[...] + t[2 * own : 2 * own + 1] * direction[...]
    new_product[...] = t[2 * own + 1 : 2 * own + 2]


def exchange(pieces, axes):
    return lax.all_to_all(pieces, axes, split_axis=0, concat_axis=0, tiled=True)


def per_device(
    points,
    source_ids,
    source_shift,
    noise_level,
    weight_in,
    bias_in,
    weight_out,
    inverse_scale,
    frequency,
    phase_shift,
    solution,
    residual,
    direction,
    prior_product,
):
    row, col = lax.axis_size(ROW), lax.axis_size(COL)
    own, columns = direction.shape
    rank = frequency.shape[1]
    groups = own // 8
    share = columns // col
    count = own * col
    to_row, to_col, waves = call(
        features_kernel,
        (shape(own + 16, 128), shape(col, 8, 256), shape(rank + 16, 256, dtype=BF16)),
        points,
        source_ids.reshape(1, own),
        source_shift,
        noise_level.reshape(1, -1),
        weight_in,
        bias_in.reshape(1, -1),
        weight_out.T,
        inverse_scale.reshape(1, -1),
        frequency,
        phase_shift.reshape(1, -1),
        residual,
        direction,
        prior_product.reshape(1, -1),
        far=range(13),
        sent=(1,),
    )
    from_col = exchange(to_col, COL)
    from_row = lax.all_gather(to_row, ROW, axis=0, tiled=False)
    piece = 3 * rank // 2 // row
    noise_row, prior, basis_t, capacity = call(
        basis_kernel,
        (shape(1, count), shape(share, 1), shape(rank, count), shape(row, piece, rank // 2)),
        from_col,
        waves,
        flops=6_000_000_000,
        sent=(3,),
        scratch=[pltpu.VMEM((col, groups, 8, 128), F32)],
    )
    parts = exchange(capacity, ROW)
    products, two_t = call(
        products_kernel,
        (shape(col, share, count), shape(2 * share, count)),
        from_row,
        from_col,
        flops=6_000_000_000,
        sent=(0,),
        scratch=[
            pltpu.VMEM((row, groups, 8, 128), F32),
            pltpu.VMEM((col, groups, 8, 128), F32),
        ],
    )
    products = exchange(products, COL)
    own_rows = call(whole_kernel, shape(piece, rank // 2), parts)
    blocks = lax.all_gather(own_rows, ROW, axis=0, tiled=True)
    image, sums = call(
        sums_kernel,
        (shape(share, count), shape(row, 2 * share, rank + 128)),
        products,
        two_t,
        noise_row,
        basis_t,
        sent=(1,),
    )
    sums = exchange(sums, ROW)
    begun, gram = call(
        early_kernel, (shape(rank, rank), shape(rank, rank)), blocks, flops=3_000_000_000
    )
    inverse = call(
        inverse_kernel,
        shape(rank, rank),
        begun,
        flops=12_000_000_000,
    )
    results = call(
        solve_kernel,
        shape(col, share, 128),
        sums,
        prior,
        inverse,
        gram,
        two_t,
        noise_row,
        basis_t,
        image,
    )
    results = exchange(results, COL)
    new_solution, new_residual, new_direction, new_product = call(
        finish_kernel,
        (shape(own, columns), shape(own, columns), shape(own, columns), shape(1, columns)),
        results.reshape(columns, 128),
        solution,
        direction,
        sent=(0, 1, 2),
    )
    return new_solution, new_residual, new_direction, new_product.reshape(columns)


def solution(mesh):
    row, col = mesh.devices.shape
    split = Mesh(mesh.devices.reshape(row // 2, 2, col // 8, 8), ROW_COL)
    lines = P(ROW_COL, None)
    placed = (lines, P(ROW_COL)) + (P(),) * 8 + (lines, lines, lines, P())
    return jax.shard_map(
        per_device,
        mesh=split,
        in_specs=placed,
        out_specs=(lines, lines, lines, P()),
        check_vma=False,
    )
```

```python
import math

import jax
import jax.numpy as jnp
from jax import lax
from jax.experimental import pallas as pl
from jax.experimental.pallas import tpu as pltpu
from jax.sharding import Mesh
from jax.sharding import PartitionSpec as P

ROW = ("y", "core")
COL = ("x", "z")
ROW_COL = ROW + COL
HIGH = lax.Precision.HIGHEST
F32 = jnp.float32
BF16 = jnp.bfloat16
NN = (((1,), (0,)), ((), ()))
NT = (((1,), (1,)), ((), ()))

def call(kernel, outs, *args, flops=1_000_000, scratch=(), far=(), sent=()):
    vmem, hbm = pl.BlockSpec(memory_space=pltpu.VMEM), pl.BlockSpec(memory_space=pltpu.HBM)
    flat = outs if isinstance(outs, tuple) else (outs,)
    far, sent = list(far), list(sent)
    copied = [args[i] for i in far] + [flat[i] for i in sent]

    def body(*refs):
        ins, res = list(refs[: len(args)]), list(refs[len(args) : len(args) + len(flat)])
        rest = refs[len(args) + len(flat) :]
        rest, held = rest[: len(scratch)], rest[len(scratch) :]
        if not copied:
            return kernel(*ins, *res, *rest)
        held, done = held[:-1], held[-1]
        into = [pltpu.make_async_copy(ins[i], held[n], done.at[n]) for n, i in enumerate(far)]
        for copy in into:
            copy.start()
        for n, i in enumerate(far):
            ins[i] = held[n]
        out = []
        for n, i in enumerate(sent, len(far)):
            out.append(pltpu.make_async_copy(held[n], res[i], done.at[n]))
            res[i] = held[n]
        for copy in into:
            copy.wait()
        kernel(*ins, *res, *rest)
        for copy in out:
            copy.start()
        for copy in out:
            copy.wait()

    extra = [pltpu.VMEM(a.shape, a.dtype) for a in copied]
    if copied:
        extra.append(pltpu.SemaphoreType.DMA((len(copied),)))
    args = [pltpu.with_memory_space_constraint(a, pltpu.HBM) if i in far else a for i, a in enumerate(args)]
    results = pl.pallas_call(
        body,
        out_shape=flat,
        in_specs=[hbm if i in far else vmem for i in range(len(args))],
        out_specs=tuple(hbm if i in sent else vmem for i in range(len(flat))),
        scratch_shapes=list(scratch) + extra,
        compiler_params=pltpu.CompilerParams(vmem_limit_bytes=16 * 2**20),
        cost_estimate=pl.CostEstimate(flops=flops, bytes_accessed=100_000, transcendentals=0),
    )(*args)
    return results if isinstance(outs, tuple) else results[0]


def shape(*dims, dtype=F32):
    return jax.ShapeDtypeStruct(dims, dtype)


def dot(a, b, dims=NN):
    return lax.dot_general(a, b, dims, precision=HIGH, preferred_element_type=F32)


def dot16(a, b, dims=NN):
    return lax.dot_general(a, b, dims, preferred_element_type=F32)


def three(x):
    h = x.astype(BF16).astype(F32)
    m = (x - h).astype(BF16).astype(F32)
    return h, m, (x - h - m).astype(BF16).astype(F32)


def stacked(x, b, dims):
    b3 = [part.astype(BF16) for part in three(b)]
    h, m, l = three(x)
    none = jnp.zeros_like(x)
    by_h = dot16(jnp.concatenate([h, m, l, none], axis=0).astype(BF16), b3[0], dims)
    by_m = dot16(jnp.concatenate([h, m], axis=0).astype(BF16), b3[1], dims)
    by_l = dot16(jnp.concatenate([h, none], axis=0).astype(BF16), b3[2], dims)
    return by_h[0:8] + (by_h[8:16] + by_m[0:8] + (by_h[16:24] + by_m[8:16] + by_l[0:8]))


def shifted_by(x, lanes):
    return pltpu.roll(x, lanes, 1)


def left_side(x):
    h, m, l = three(x)
    one = h + shifted_by(h, 42) + shifted_by(m, 84)
    two = h + shifted_by(l, 42) + shifted_by(m, 84)
    return jnp.concatenate([one, two], axis=1).astype(BF16)


def right_side(x):
    h, m, l = three(x)
    one = h + shifted_by(m, 42) + shifted_by(h, 84)
    two = l + shifted_by(h, 42) + shifted_by(m, 84)
    return jnp.concatenate([one, two], axis=1).astype(BF16)


def cosine(turns, scale):
    t = 0.25 - jnp.abs(turns - jnp.floor(turns + 0.5))
    s = t * t
    p = 0.0
    for k in range(5, -1, -1):
        c = (-1) ** k * scale * (2.0 * math.pi) ** (2 * k + 1) / math.factorial(2 * k + 1)
        p = p * s + c
    return p * t


def lane_of(rows, lanes=128):
    return lax.broadcasted_iota(jnp.int32, (rows, lanes), 1)


def features_kernel(
    points, ids, shift, level, w_in, b_in, w_out_t, inv, freq, phase, res, drn, prior, to_row, to_col, waves
):
    own = points.shape[0]
    groups = own // 8
    sources = shift.shape[0]
    hot_t = (lax.broadcasted_iota(jnp.int32, (sources, own), 0) == ids[...]).astype(F32)
    hot = hot_t.T
    shifted = points[...] + dot(hot, shift[...])
    hidden = jnp.tanh(dot(shifted, w_in[...]) + b_in[...])
    f = dot(hidden, w_out_t[...], NT) * inv[...]
    n = -0.5 * jnp.sum(f * f, axis=1, keepdims=True)
    noise = dot(hot, jnp.broadcast_to(level[...], (8, sources)), NT)[:, 0:1]
    first = jnp.concatenate([f[8 * g : 8 * g + 8] for g in range(4)], axis=1)
    second = jnp.concatenate(
        [f[8 * g : 8 * g + 8] for g in range(4, groups)]
        + [jnp.zeros((8, own), F32)]
        + [x[8 * g : 8 * g + 8] for g in range(groups) for x in (n, noise)]
        + [jnp.zeros((8, 128 - 32 - own - 2 * groups), F32)],
        axis=1,
    )
    to_row[0:own, :] = drn[...]
    to_row[own : own + 8, :] = first
    to_row[own + 8 : own + 16, :] = second
    col = to_col.shape[0]
    share = res.shape[1] // col

    def turned(x):
        low, high = jnp.zeros((32, 128), F32), jnp.zeros((128 - 32 - own, 128), F32)
        return jnp.concatenate([low, x, high], axis=0).T

    prior_t = jnp.broadcast_to(prior[...], (128, 128)).T
    res_t = jnp.where(lane_of(128) == 32 + own + 2 * groups, prior_t, turned(res[...]))
    drn_t = turned(drn[...])
    spare = [jnp.zeros((8 - 2 * share, 128), F32)] if share < 4 else []
    for c in range(col):
        at = slice(c * share, (c + 1) * share)
        to_col[c, :, 0:128] = first
        to_col[c, :, 128:256] = second + jnp.concatenate([res_t[at], drn_t[at]] + spare, axis=0)
    feat = freq.shape[0]
    rank = freq.shape[1]
    table = jnp.concatenate(
        [
            freq[...],
            jnp.zeros((2, rank), F32),
            phase[...],
            jnp.zeros((128 - feat - 3, rank), F32),
        ],
        axis=0,
    ).T
    pick = jnp.where(lane_of(waves.shape[0] - rank) == feat + 1, 1.0, 0.0)
    waves[...] = right_side(jnp.concatenate([table * (0.5 / math.pi), pick], axis=0))


def unpacked(first, second, x):
    groups = x.shape[1]
    own = groups * 8
    for g in range(groups):
        source = first[:, :, 32 * g : 32 * g + 32] if g < 4 else second[:, :, 32 * g - 128 : 32 * g - 96]
        x[:, g, :, 0:32] = source
        at = 32 + own + 2 * g
        x[:, g, :, 32:34] = second[:, :, at : at + 2]
    return x[...].reshape(x.shape[0] * own, 128)


def row_side(arrived, x):
    values = unpacked(arrived[:, :, 0:128], arrived[:, :, 128:256], x)
    lane = lane_of(values.shape[0])
    return left_side(jnp.where(lane < 34, values, jnp.where(lane == 34, 1.0, 0.0)))


def basis_kernel(arrived, waves, noise_row, prior, basis_t, capacity, x):
    groups = x.shape[1]
    own = groups * 8
    share = prior.shape[0]
    side = row_side(arrived, x)
    at = 160 + own + 2 * groups
    prior[...] = arrived[0, 0:share, at : at + 1]
    rank = basis_t.shape[0]
    half = rank // 2
    turned = dot16(waves[...], side, NT)
    noise = turned[rank : rank + 1]
    noise_row[...] = noise
    basis = cosine(turned[0:rank], math.sqrt(2.0 / rank))
    basis_t[...] = basis
    weighted = basis * (1.0 / noise)
    full = dot(weighted, basis, NT)
    blocks = jnp.concatenate([full[:, 0:half], full[half:, half:]], axis=0)
    capacity[...] = blocks.reshape(capacity.shape)


def products_kernel(arrived, from_col, out, two_t, x, x_col):
    pieces, groups = x.shape[0], x.shape[1]
    own = groups * 8
    col, share = out.shape[0], out.shape[1]
    values = unpacked(arrived[:, own : own + 8, :], arrived[:, own + 8 : own + 16, :], x)
    lane = lane_of(values.shape[0])
    norm = jnp.where(lane == 32, values, 0.0)
    values = jnp.where(lane < 32, values, jnp.where(lane == 32, 1.0, 0.0)) + shifted_by(norm, 2)
    j_side = right_side(values)
    d_t = arrived[:, 0:own, :].reshape(pieces * own, 128).T
    high = d_t.astype(BF16)
    low = (d_t - high.astype(F32)).astype(BF16)
    both = jnp.concatenate([high, low], axis=0)
    i_side = row_side(from_col, x_col)
    for c in range(col):
        two_t[:, own * c : own * (c + 1)] = from_col[c, 0 : 2 * share, 160 : 160 + own]
    count = i_side.shape[0]
    step = 256
    for i in range(count // step):
        k = jnp.exp(dot16(j_side, i_side[i * step : (i + 1) * step, :], NT))
        k_high = k.astype(BF16)
        k_low = (k - k_high.astype(F32)).astype(BF16)
        pair = dot16(both, k_high)
        total = pair[0:128] + (pair[128:256] + dot16(high, k_low))
        for c in range(col):
            out[c, :, i * step : (i + 1) * step] = total[share * c : share * (c + 1)]


def whole_kernel(parts, out):
    out[...] = jnp.sum(parts[...], axis=0)


def eliminated(p, base, lane, one_lane, sub):
    size, rank = p.shape
    for t in range(0, size, 4):
        j = base + t
        c = [jnp.broadcast_to(p[:, j + i : j + i + 1], (size, rank)) for i in range(4)]
        s = [[c[i][t + q : t + q + 1] for q in range(4)] for i in range(4)]
        inside = (one_lane >= j) & (one_lane < j + 4)
        r = [
            jnp.where(inside, jnp.where(one_lane == j + i, 1.0, 0.0), p[t + i : t + i + 1])
            for i in range(4)
        ]
        inv = 1.0 / (s[0][0] * s[1][1] - s[0][1] * s[0][1])
        a0, a1, a2 = s[1][1] * inv, -s[0][1] * inv, s[0][0] * inv
        g02, g03 = a0 * s[2][0] + a1 * s[2][1], a0 * s[3][0] + a1 * s[3][1]
        g12, g13 = a1 * s[2][0] + a2 * s[2][1], a1 * s[3][0] + a2 * s[3][1]
        e = s[2][2] - s[2][0] * g02 - s[2][1] * g12
        f = s[3][2] - s[2][0] * g03 - s[2][1] * g13
        h = s[3][3] - s[3][0] * g03 - s[3][1] * g13
        inv = 1.0 / (e * h - f * f)
        e, f, h = h * inv, -f * inv, e * inv
        v2 = r[2] - g02 * r[0] - g12 * r[1]
        v3 = r[3] - g03 * r[0] - g13 * r[1]
        u2 = e * v2 + f * v3
        u3 = f * v2 + h * v3
        u0 = a0 * r[0] + a1 * r[1] - g02 * u2 - g03 * u3
        u1 = a1 * r[0] + a2 * r[1] - g12 * u2 - g13 * u3
        here = (sub >= t) & (sub < t + 4)
        p = jnp.where(((lane < j) | (lane >= j + 4)) & ~here, p, 0.0)
        for i, u in enumerate((u0, u1, u2, u3)):
            p = p - jnp.where(here, jnp.where(sub == t + i, -1.0, 0.0), c[i]) * u
    return p


def inverse_kernel(blocks, out, gram):
    rank = out.shape[0]
    size = 32
    rows = lax.broadcasted_iota(jnp.int32, (rank, rank), 0)
    cols = lax.broadcasted_iota(jnp.int32, (rank, rank), 1)
    half = rank // 2
    one, two, three_ = blocks[0:half], blocks[half:rank], blocks[rank : rank + half]
    m = jnp.concatenate(
        [jnp.concatenate([one, two.T], axis=1), jnp.concatenate([two, three_], axis=1)], axis=0
    )
    m = m + jnp.where(rows == cols, 1.0, 0.0)
    gram[...] = m
    count = rank // size
    panels = [m[i * size : (i + 1) * size] for i in range(count)]
    lane, one_lane = lane_of(size, rank), lane_of(1, rank)
    sub = lax.broadcasted_iota(jnp.int32, (size, rank), 0)
    for k in range(count):
        base = k * size
        p = eliminated(panels[k], base, lane, one_lane, sub)
        panels[k] = p

        def updated(x):
            at = lane_of(x.shape[0], rank)
            inside = (at >= base) & (at < base + size)
            return jnp.where(inside, 0.0, x) - dot(x[:, base : base + size], p)

        others = [i for i in range(count) if i != k]
        if k + 1 < count:
            panels[k + 1] = updated(panels[k + 1])
            others.remove(k + 1)
        rest = updated(jnp.concatenate([panels[i] for i in others], axis=0))
        for w, i in enumerate(others):
            panels[i] = rest[w * size : (w + 1) * size]
    for i in range(count):
        out[i * size : (i + 1) * size] = panels[i]


def sums_kernel(arrived, two_t, noise_row, basis_t, image, out):
    share = image.shape[0]
    res, drn = two_t[0:share], two_t[share : 2 * share]
    noise = noise_row[...]
    value = jnp.sum(arrived[...], axis=0) + noise * drn
    image[...] = value
    stack = jnp.concatenate([res, value], axis=0)
    scaled = stack * (1.0 / noise)
    proj = stacked(scaled, basis_t[...], NT)
    over = scaled[share:]
    left = jnp.concatenate(
        [jnp.sum(res * scaled[0:share], axis=1, keepdims=True), jnp.sum(value * over, axis=1, keepdims=True)],
        axis=0,
    )
    right = jnp.concatenate(
        [jnp.sum(drn * value, axis=1, keepdims=True), jnp.sum(res * over, axis=1, keepdims=True)],
        axis=0,
    )
    lane = lane_of(2 * share)
    scalars = jnp.where(lane == 0, left, jnp.where(lane == 1, right, 0.0))
    rank = proj.shape[1]
    for r in range(out.shape[0]):
        out[r, :, 0:rank] = proj
        out[r, :, rank : rank + 128] = scalars


def solve_kernel(arrived, prior, inverse, gram, two_t, noise_row, basis_t, image, out):
    share = image.shape[0]
    rank = gram.shape[0]
    res, drn = two_t[0:share], two_t[share : 2 * share]
    total = jnp.sum(arrived[...], axis=0)
    scalars = total[:, rank : rank + 2]
    res_res, curvature = scalars[0:share, 0:1], scalars[0:share, 1:2]
    img_img, res_img = scalars[share : 2 * share, 0:1], scalars[share : 2 * share, 1:2]
    alpha = prior[...] / curvature
    projected = total[0:share, 0:rank] - alpha * total[share : 2 * share, 0:rank]
    coeffs = dot(projected, inverse[...])
    coeffs = coeffs + dot(projected - dot(coeffs, gram[...]), inverse[...])
    norm = res_res - 2.0 * alpha * res_img + alpha * alpha * img_img
    product = norm - jnp.sum(projected * coeffs, axis=1, keepdims=True)
    new_res = res - alpha * image[...]
    padded = jnp.concatenate([coeffs, jnp.zeros((8 - share, rank), F32)], axis=0)
    precond = (new_res - stacked(padded, basis_t[...], NN)[0:share]) * (1.0 / noise_row[...])
    new_drn = precond + product / prior[...] * drn
    pieces = out.shape[0]
    own = new_res.shape[1] // pieces
    spare = jnp.zeros((share, 128 - 2 * own - 2), F32)
    for c in range(pieces):
        at = slice(c * own, (c + 1) * own)
        out[c] = jnp.concatenate([new_res[:, at], new_drn[:, at], alpha, product, spare], axis=1)


def finish_kernel(arrived, solution, direction, new_solution, new_residual, new_direction, new_product):
    own = solution.shape[0]
    t = arrived[...].T
    new_residual[...] = t[0:own]
    new_direction[...] = t[own : 2 * own]
    new_solution[...] = solution[...] + t[2 * own : 2 * own + 1] * direction[...]
    new_product[...] = t[2 * own + 1 : 2 * own + 2]


def exchange(pieces, axes):
    return lax.all_to_all(pieces, axes, split_axis=0, concat_axis=0, tiled=True)


def per_device(
    points,
    source_ids,
    source_shift,
    noise_level,
    weight_in,
    bias_in,
    weight_out,
    inverse_scale,
    frequency,
    phase_shift,
    solution,
    residual,
    direction,
    prior_product,
):
    row, col = lax.axis_size(ROW), lax.axis_size(COL)
    own, columns = direction.shape
    rank = frequency.shape[1]
    groups = own // 8
    share = columns // col
    count = own * col
    to_row, to_col, waves = call(
        features_kernel,
        (shape(own + 16, 128), shape(col, 8, 256), shape(rank + 16, 256, dtype=BF16)),
        points,
        source_ids.reshape(1, own),
        source_shift,
        noise_level.reshape(1, -1),
        weight_in,
        bias_in.reshape(1, -1),
        weight_out.T,
        inverse_scale.reshape(1, -1),
        frequency,
        phase_shift.reshape(1, -1),
        residual,
        direction,
        prior_product.reshape(1, -1),
        far=range(13),
        sent=(1,),
    )
    from_col = exchange(to_col, COL)
    piece = 3 * rank // 2 // row
    noise_row, prior, basis_t, capacity = call(
        basis_kernel,
        (shape(1, count), shape(share, 1), shape(rank, count), shape(row, piece, rank // 2)),
        from_col,
        waves,
        flops=6_000_000_000,
        sent=(3,),
        scratch=[pltpu.VMEM((col, groups, 8, 128), F32)],
    )
    to_row, capacity = lax.optimization_barrier((to_row, capacity))
    parts = exchange(capacity, ROW)
    from_row = lax.all_gather(to_row, ROW, axis=0, tiled=False)
    products, two_t = call(
        products_kernel,
        (shape(col, share, count), shape(2 * share, count)),
        from_row,
        from_col,
        flops=1_000,
        sent=(0,),
        scratch=[
            pltpu.VMEM((row, groups, 8, 128), F32),
            pltpu.VMEM((col, groups, 8, 128), F32),
        ],
    )
    products = exchange(products, COL)
    own_rows = call(whole_kernel, shape(piece, rank // 2), parts)
    blocks = lax.all_gather(own_rows, ROW, axis=0, tiled=True)
    image, sums = call(
        sums_kernel,
        (shape(share, count), shape(row, 2 * share, rank + 128)),
        products,
        two_t,
        noise_row,
        basis_t,
        sent=(1,),
    )
    sums = exchange(sums, ROW)
    inverse, gram = call(
        inverse_kernel,
        (shape(rank, rank), shape(rank, rank)),
        blocks,
        flops=12_000_000_000,
    )
    results = call(
        solve_kernel,
        shape(col, share, 128),
        sums,
        prior,
        inverse,
        gram,
        two_t,
        noise_row,
        basis_t,
        image,
    )
    results = exchange(results, COL)
    new_solution, new_residual, new_direction, new_product = call(
        finish_kernel,
        (shape(own, columns), shape(own, columns), shape(own, columns), shape(1, columns)),
        results.reshape(columns, 128),
        solution,
        direction,
        sent=(0, 1, 2),
    )
    return new_solution, new_residual, new_direction, new_product.reshape(columns)


def solution(mesh):
    row, col = mesh.devices.shape
    split = Mesh(mesh.devices.reshape(row // 2, 2, col // 8, 8), ROW_COL)
    lines = P(ROW_COL, None)
    placed = (lines, P(ROW_COL)) + (P(),) * 8 + (lines, lines, lines, P())
    return jax.shard_map(
        per_device,
        mesh=split,
        in_specs=placed,
        out_specs=(lines, lines, lines, P()),
        check_vma=False,
    )
```

```python
import math

import jax
import jax.numpy as jnp
from jax import lax
from jax.experimental import pallas as pl
from jax.experimental.pallas import tpu as pltpu
from jax.sharding import Mesh
from jax.sharding import PartitionSpec as P

ROW = ("y", "core")
COL = ("x", "z")
ROW_COL = ROW + COL
HIGH = lax.Precision.HIGHEST
F32 = jnp.float32
BF16 = jnp.bfloat16
NN = (((1,), (0,)), ((), ()))
NT = (((1,), (1,)), ((), ()))

def call(kernel, outs, *args, flops=1_000_000, scratch=(), far=(), sent=(), early=False):
    vmem, hbm = pl.BlockSpec(memory_space=pltpu.VMEM), pl.BlockSpec(memory_space=pltpu.HBM)
    flat = outs if isinstance(outs, tuple) else (outs,)
    far, sent = list(far), list(sent)
    copied = [args[i] for i in far] + [flat[i] for i in sent]

    def body(*refs):
        ins, res = list(refs[: len(args)]), list(refs[len(args) : len(args) + len(flat)])
        rest = refs[len(args) + len(flat) :]
        rest, held = rest[: len(scratch)], rest[len(scratch) :]
        if not copied:
            return kernel(*ins, *res, *rest)
        held, done = held[:-1], held[-1]
        into = [pltpu.make_async_copy(ins[i], held[n], done.at[n]) for n, i in enumerate(far)]
        for copy in into:
            copy.start()
        for n, i in enumerate(far):
            ins[i] = held[n]
        out = []
        for n, i in enumerate(sent, len(far)):
            out.append(pltpu.make_async_copy(held[n], res[i], done.at[n]))
            res[i] = held[n]
        for copy in into:
            copy.wait()

        def send():
            for copy in out:
                copy.start()

        if early:
            kernel(*ins, *res, *rest, send)
        else:
            kernel(*ins, *res, *rest)
            send()
        for copy in out:
            copy.wait()

    extra = [pltpu.VMEM(a.shape, a.dtype) for a in copied]
    if copied:
        extra.append(pltpu.SemaphoreType.DMA((len(copied),)))
    args = [pltpu.with_memory_space_constraint(a, pltpu.HBM) if i in far else a for i, a in enumerate(args)]
    results = pl.pallas_call(
        body,
        out_shape=flat,
        in_specs=[hbm if i in far else vmem for i in range(len(args))],
        out_specs=tuple(hbm if i in sent else vmem for i in range(len(flat))),
        scratch_shapes=list(scratch) + extra,
        compiler_params=pltpu.CompilerParams(vmem_limit_bytes=16 * 2**20),
        cost_estimate=pl.CostEstimate(flops=flops, bytes_accessed=100_000, transcendentals=0),
    )(*args)
    return results if isinstance(outs, tuple) else results[0]


def shape(*dims, dtype=F32):
    return jax.ShapeDtypeStruct(dims, dtype)


def dot(a, b, dims=NN):
    return lax.dot_general(a, b, dims, precision=HIGH, preferred_element_type=F32)


def dot16(a, b, dims=NN):
    return lax.dot_general(a, b, dims, preferred_element_type=F32)


def three(x):
    h = x.astype(BF16).astype(F32)
    m = (x - h).astype(BF16).astype(F32)
    return h, m, (x - h - m).astype(BF16).astype(F32)


def stacked(x, b, dims):
    b3 = [part.astype(BF16) for part in three(b)]
    h, m, l = three(x)
    none = jnp.zeros_like(x)
    by_h = dot16(jnp.concatenate([h, m, l, none], axis=0).astype(BF16), b3[0], dims)
    by_m = dot16(jnp.concatenate([h, m], axis=0).astype(BF16), b3[1], dims)
    by_l = dot16(jnp.concatenate([h, none], axis=0).astype(BF16), b3[2], dims)
    return by_h[0:8] + (by_h[8:16] + by_m[0:8] + (by_h[16:24] + by_m[8:16] + by_l[0:8]))


def shifted_by(x, lanes):
    return pltpu.roll(x, lanes, 1)


def left_side(x):
    h, m, l = three(x)
    one = h + shifted_by(h, 42) + shifted_by(m, 84)
    two = h + shifted_by(l, 42) + shifted_by(m, 84)
    return jnp.concatenate([one, two], axis=1).astype(BF16)


def right_side(x):
    h, m, l = three(x)
    one = h + shifted_by(m, 42) + shifted_by(h, 84)
    two = l + shifted_by(h, 42) + shifted_by(m, 84)
    return jnp.concatenate([one, two], axis=1).astype(BF16)


def cosine(turns, scale):
    t = 0.25 - jnp.abs(turns - jnp.floor(turns + 0.5))
    s = t * t
    p = 0.0
    for k in range(5, -1, -1):
        c = (-1) ** k * scale * (2.0 * math.pi) ** (2 * k + 1) / math.factorial(2 * k + 1)
        p = p * s + c
    return p * t


def lane_of(rows, lanes=128):
    return lax.broadcasted_iota(jnp.int32, (rows, lanes), 1)


def features_kernel(
    points, ids, shift, level, w_in, b_in, w_out_t, inv, freq, phase, res, drn, prior, to_row, to_col, waves, send
):
    own = points.shape[0]
    groups = own // 8
    sources = shift.shape[0]
    hot_t = (lax.broadcasted_iota(jnp.int32, (sources, own), 0) == ids[...]).astype(F32)
    hot = hot_t.T
    shifted = points[...] + dot(hot, shift[...])
    hidden = jnp.tanh(dot(shifted, w_in[...]) + b_in[...])
    f = dot(hidden, w_out_t[...], NT) * inv[...]
    n = -0.5 * jnp.sum(f * f, axis=1, keepdims=True)
    noise = dot(hot, jnp.broadcast_to(level[...], (8, sources)), NT)[:, 0:1]
    first = jnp.concatenate([f[8 * g : 8 * g + 8] for g in range(4)], axis=1)
    second = jnp.concatenate(
        [f[8 * g : 8 * g + 8] for g in range(4, groups)]
        + [jnp.zeros((8, own), F32)]
        + [x[8 * g : 8 * g + 8] for g in range(groups) for x in (n, noise)]
        + [jnp.zeros((8, 128 - 32 - own - 2 * groups), F32)],
        axis=1,
    )
    to_row[0:own, :] = drn[...]
    to_row[own : own + 8, :] = first
    to_row[own + 8 : own + 16, :] = second
    col = to_col.shape[0]
    share = res.shape[1] // col

    def turned(x):
        low, high = jnp.zeros((32, 128), F32), jnp.zeros((128 - 32 - own, 128), F32)
        return jnp.concatenate([low, x, high], axis=0).T

    prior_t = jnp.broadcast_to(prior[...], (128, 128)).T
    res_t = jnp.where(lane_of(128) == 32 + own + 2 * groups, prior_t, turned(res[...]))
    drn_t = turned(drn[...])
    spare = [jnp.zeros((8 - 2 * share, 128), F32)] if share < 4 else []
    for c in range(col):
        at = slice(c * share, (c + 1) * share)
        to_col[c, :, 0:128] = first
        to_col[c, :, 128:256] = second + jnp.concatenate([res_t[at], drn_t[at]] + spare, axis=0)
    send()
    feat = freq.shape[0]
    rank = freq.shape[1]
    table = jnp.concatenate(
        [
            freq[...],
            jnp.zeros((2, rank), F32),
            phase[...],
            jnp.zeros((128 - feat - 3, rank), F32),
        ],
        axis=0,
    ).T
    pick = jnp.where(lane_of(waves.shape[0] - rank) == feat + 1, 1.0, 0.0)
    waves[...] = right_side(jnp.concatenate([table * (0.5 / math.pi), pick], axis=0))


def unpacked(first, second, x):
    groups = x.shape[1]
    own = groups * 8
    for g in range(groups):
        source = first[:, :, 32 * g : 32 * g + 32] if g < 4 else second[:, :, 32 * g - 128 : 32 * g - 96]
        x[:, g, :, 0:32] = source
        at = 32 + own + 2 * g
        x[:, g, :, 32:34] = second[:, :, at : at + 2]
    return x[...].reshape(x.shape[0] * own, 128)


def row_side(arrived, x):
    values = unpacked(arrived[:, :, 0:128], arrived[:, :, 128:256], x)
    lane = lane_of(values.shape[0])
    return left_side(jnp.where(lane < 34, values, jnp.where(lane == 34, 1.0, 0.0)))


def basis_kernel(arrived, waves, noise_row, prior, basis_t, capacity, x):
    groups = x.shape[1]
    own = groups * 8
    share = prior.shape[0]
    side = row_side(arrived, x)
    at = 160 + own + 2 * groups
    prior[...] = arrived[0, 0:share, at : at + 1]
    rank = basis_t.shape[0]
    half = rank // 2
    turned = dot16(waves[...], side, NT)
    noise = turned[rank : rank + 1]
    noise_row[...] = noise
    basis = cosine(turned[0:rank], math.sqrt(2.0 / rank))
    basis_t[...] = basis
    weighted = basis * (1.0 / noise)
    full = dot(weighted, basis, NT)
    blocks = jnp.concatenate([full[:, 0:half], full[half:, half:]], axis=0)
    capacity[...] = blocks.reshape(capacity.shape)


def products_kernel(arrived, from_col, out, two_t, x, x_col):
    pieces, groups = x.shape[0], x.shape[1]
    own = groups * 8
    col, share = out.shape[0], out.shape[1]
    values = unpacked(arrived[:, own : own + 8, :], arrived[:, own + 8 : own + 16, :], x)
    lane = lane_of(values.shape[0])
    norm = jnp.where(lane == 32, values, 0.0)
    values = jnp.where(lane < 32, values, jnp.where(lane == 32, 1.0, 0.0)) + shifted_by(norm, 2)
    j_side = right_side(values)
    d_t = arrived[:, 0:own, :].reshape(pieces * own, 128).T
    high = d_t.astype(BF16)
    low = (d_t - high.astype(F32)).astype(BF16)
    both = jnp.concatenate([high, low], axis=0)
    i_side = row_side(from_col, x_col)
    for c in range(col):
        two_t[:, own * c : own * (c + 1)] = from_col[c, 0 : 2 * share, 160 : 160 + own]
    count = i_side.shape[0]
    step = 256
    for i in range(count // step):
        k = jnp.exp(dot16(j_side, i_side[i * step : (i + 1) * step, :], NT))
        k_high = k.astype(BF16)
        k_low = (k - k_high.astype(F32)).astype(BF16)
        pair = dot16(both, k_high)
        total = pair[0:128] + (pair[128:256] + dot16(high, k_low))
        for c in range(col):
            out[c, :, i * step : (i + 1) * step] = total[share * c : share * (c + 1)]


def whole_kernel(parts, out):
    out[...] = jnp.sum(parts[...], axis=0)


def eliminated(p, base, lane, one_lane, sub):
    size, rank = p.shape
    for t in range(0, size, 4):
        j = base + t
        c = [jnp.broadcast_to(p[:, j + i : j + i + 1], (size, rank)) for i in range(4)]
        s = [[c[i][t + q : t + q + 1] for q in range(4)] for i in range(4)]
        inside = (one_lane >= j) & (one_lane < j + 4)
        r = [
            jnp.where(inside, jnp.where(one_lane == j + i, 1.0, 0.0), p[t + i : t + i + 1])
            for i in range(4)
        ]
        inv = 1.0 / (s[0][0] * s[1][1] - s[0][1] * s[0][1])
        a0, a1, a2 = s[1][1] * inv, -s[0][1] * inv, s[0][0] * inv
        g02, g03 = a0 * s[2][0] + a1 * s[2][1], a0 * s[3][0] + a1 * s[3][1]
        g12, g13 = a1 * s[2][0] + a2 * s[2][1], a1 * s[3][0] + a2 * s[3][1]
        e = s[2][2] - s[2][0] * g02 - s[2][1] * g12
        f = s[3][2] - s[2][0] * g03 - s[2][1] * g13
        h = s[3][3] - s[3][0] * g03 - s[3][1] * g13
        inv = 1.0 / (e * h - f * f)
        e, f, h = h * inv, -f * inv, e * inv
        v2 = r[2] - g02 * r[0] - g12 * r[1]
        v3 = r[3] - g03 * r[0] - g13 * r[1]
        u2 = e * v2 + f * v3
        u3 = f * v2 + h * v3
        u0 = a0 * r[0] + a1 * r[1] - g02 * u2 - g03 * u3
        u1 = a1 * r[0] + a2 * r[1] - g12 * u2 - g13 * u3
        here = (sub >= t) & (sub < t + 4)
        p = jnp.where(((lane < j) | (lane >= j + 4)) & ~here, p, 0.0)
        for i, u in enumerate((u0, u1, u2, u3)):
            p = p - jnp.where(here, jnp.where(sub == t + i, -1.0, 0.0), c[i]) * u
    return p


def inverse_kernel(blocks, out, gram):
    rank = out.shape[0]
    size = 32
    rows = lax.broadcasted_iota(jnp.int32, (rank, rank), 0)
    cols = lax.broadcasted_iota(jnp.int32, (rank, rank), 1)
    half = rank // 2
    one, two, three_ = blocks[0:half], blocks[half:rank], blocks[rank : rank + half]
    m = jnp.concatenate(
        [jnp.concatenate([one, two.T], axis=1), jnp.concatenate([two, three_], axis=1)], axis=0
    )
    m = m + jnp.where(rows == cols, 1.0, 0.0)
    gram[...] = m
    count = rank // size
    panels = [m[i * size : (i + 1) * size] for i in range(count)]
    lane, one_lane = lane_of(size, rank), lane_of(1, rank)
    sub = lax.broadcasted_iota(jnp.int32, (size, rank), 0)
    for k in range(count):
        base = k * size
        p = eliminated(panels[k], base, lane, one_lane, sub)
        panels[k] = p

        def updated(x):
            at = lane_of(x.shape[0], rank)
            inside = (at >= base) & (at < base + size)
            return jnp.where(inside, 0.0, x) - dot(x[:, base : base + size], p)

        others = [i for i in range(count) if i != k]
        if k + 1 < count:
            panels[k + 1] = updated(panels[k + 1])
            others.remove(k + 1)
        rest = updated(jnp.concatenate([panels[i] for i in others], axis=0))
        for w, i in enumerate(others):
            panels[i] = rest[w * size : (w + 1) * size]
    for i in range(count):
        out[i * size : (i + 1) * size] = panels[i]


def sums_kernel(arrived, two_t, noise_row, basis_t, image, out):
    share = image.shape[0]
    res, drn = two_t[0:share], two_t[share : 2 * share]
    noise = noise_row[...]
    value = jnp.sum(arrived[...], axis=0) + noise * drn
    image[...] = value
    stack = jnp.concatenate([res, value], axis=0)
    scaled = stack * (1.0 / noise)
    proj = stacked(scaled, basis_t[...], NT)
    over = scaled[share:]
    left = jnp.concatenate(
        [jnp.sum(res * scaled[0:share], axis=1, keepdims=True), jnp.sum(value * over, axis=1, keepdims=True)],
        axis=0,
    )
    right = jnp.concatenate(
        [jnp.sum(drn * value, axis=1, keepdims=True), jnp.sum(res * over, axis=1, keepdims=True)],
        axis=0,
    )
    lane = lane_of(2 * share)
    scalars = jnp.where(lane == 0, left, jnp.where(lane == 1, right, 0.0))
    rank = proj.shape[1]
    last = jnp.zeros((1, 128), F32)
    one_lane = lane_of(1)
    for i in range(2 * share):
        for k in range(2):
            last = jnp.where(one_lane == 2 * i + k, scalars[i : i + 1, k : k + 1], last)
    line = jnp.concatenate([proj[i : i + 1] for i in range(2 * share)] + [last], axis=1)
    for r in range(out.shape[0]):
        out[r] = line


def solve_kernel(arrived, prior, inverse, gram, two_t, noise_row, basis_t, image, out):
    share = image.shape[0]
    rank = gram.shape[0]
    res, drn = two_t[0:share], two_t[share : 2 * share]
    line = jnp.sum(arrived[...], axis=0)
    total = jnp.concatenate([line[:, i * rank : (i + 1) * rank] for i in range(2 * share)], axis=0)
    last = line[:, 2 * share * rank :]
    scalars = jnp.concatenate([last[:, 2 * i : 2 * i + 2] for i in range(2 * share)], axis=0)
    res_res, curvature = scalars[0:share, 0:1], scalars[0:share, 1:2]
    img_img, res_img = scalars[share : 2 * share, 0:1], scalars[share : 2 * share, 1:2]
    alpha = prior[...] / curvature
    projected = total[0:share, 0:rank] - alpha * total[share : 2 * share, 0:rank]
    coeffs = dot(projected, inverse[...])
    coeffs = coeffs + dot(projected - dot(coeffs, gram[...]), inverse[...])
    norm = res_res - 2.0 * alpha * res_img + alpha * alpha * img_img
    product = norm - jnp.sum(projected * coeffs, axis=1, keepdims=True)
    new_res = res - alpha * image[...]
    padded = jnp.concatenate([coeffs, jnp.zeros((8 - share, rank), F32)], axis=0)
    precond = (new_res - stacked(padded, basis_t[...], NN)[0:share]) * (1.0 / noise_row[...])
    new_drn = precond + product / prior[...] * drn
    pieces = out.shape[0]
    own = new_res.shape[1] // pieces
    spare = jnp.zeros((share, 128 - 2 * own - 2), F32)
    for c in range(pieces):
        at = slice(c * own, (c + 1) * own)
        out[c] = jnp.concatenate([new_res[:, at], new_drn[:, at], alpha, product, spare], axis=1)


def finish_kernel(arrived, solution, direction, new_solution, new_residual, new_direction, new_product):
    own = solution.shape[0]
    t = arrived[...].T
    new_residual[...] = t[0:own]
    new_direction[...] = t[own : 2 * own]
    new_solution[...] = solution[...] + t[2 * own : 2 * own + 1] * direction[...]
    new_product[...] = t[2 * own + 1 : 2 * own + 2]


def exchange(pieces, axes):
    return lax.all_to_all(pieces, axes, split_axis=0, concat_axis=0, tiled=True)


def per_device(
    points,
    source_ids,
    source_shift,
    noise_level,
    weight_in,
    bias_in,
    weight_out,
    inverse_scale,
    frequency,
    phase_shift,
    solution,
    residual,
    direction,
    prior_product,
):
    row, col = lax.axis_size(ROW), lax.axis_size(COL)
    own, columns = direction.shape
    rank = frequency.shape[1]
    groups = own // 8
    share = columns // col
    count = own * col
    to_row, to_col, waves = call(
        features_kernel,
        (shape(own + 16, 128), shape(col, 8, 256), shape(rank + 16, 256, dtype=BF16)),
        points,
        source_ids.reshape(1, own),
        source_shift,
        noise_level.reshape(1, -1),
        weight_in,
        bias_in.reshape(1, -1),
        weight_out.T,
        inverse_scale.reshape(1, -1),
        frequency,
        phase_shift.reshape(1, -1),
        residual,
        direction,
        prior_product.reshape(1, -1),
        far=range(13),
        sent=(1,),
        early=True,
    )
    from_col = exchange(to_col, COL)
    from_row = lax.all_gather(to_row, ROW, axis=0, tiled=False)
    piece = 3 * rank // 2 // row
    noise_row, prior, basis_t, capacity = call(
        basis_kernel,
        (shape(1, count), shape(share, 1), shape(rank, count), shape(row, piece, rank // 2)),
        from_col,
        waves,
        flops=6_000_000_000,
        sent=(3,),
        scratch=[pltpu.VMEM((col, groups, 8, 128), F32)],
    )
    parts = exchange(capacity, ROW)
    products, two_t = call(
        products_kernel,
        (shape(col, share, count), shape(2 * share, count)),
        from_row,
        from_col,
        flops=6_000_000_000,
        sent=(0,),
        scratch=[
            pltpu.VMEM((row, groups, 8, 128), F32),
            pltpu.VMEM((col, groups, 8, 128), F32),
        ],
    )
    products = exchange(products, COL)
    own_rows = call(whole_kernel, shape(piece, rank // 2), parts)
    blocks = lax.all_gather(own_rows, ROW, axis=0, tiled=True)
    image, sums = call(
        sums_kernel,
        (shape(share, count), shape(row, 1, 2 * share * rank + 128)),
        products,
        two_t,
        noise_row,
        basis_t,
        sent=(1,),
    )
    sums = exchange(sums, ROW)
    inverse, gram = call(
        inverse_kernel,
        (shape(rank, rank), shape(rank, rank)),
        blocks,
        flops=12_000_000_000,
    )
    results = call(
        solve_kernel,
        shape(col, share, 128),
        sums,
        prior,
        inverse,
        gram,
        two_t,
        noise_row,
        basis_t,
        image,
    )
    results = exchange(results, COL)
    new_solution, new_residual, new_direction, new_product = call(
        finish_kernel,
        (shape(own, columns), shape(own, columns), shape(own, columns), shape(1, columns)),
        results.reshape(columns, 128),
        solution,
        direction,
        sent=(0, 1, 2),
    )
    return new_solution, new_residual, new_direction, new_product.reshape(columns)


def solution(mesh):
    row, col = mesh.devices.shape
    split = Mesh(mesh.devices.reshape(row // 2, 2, col // 8, 8), ROW_COL)
    lines = P(ROW_COL, None)
    placed = (lines, P(ROW_COL)) + (P(),) * 8 + (lines, lines, lines, P())
    return jax.shard_map(
        per_device,
        mesh=split,
        in_specs=placed,
        out_specs=(lines, lines, lines, P()),
        check_vma=False,
    )
```
